32 devices in a mesh: seq: 8 (over y, x, core), fsdp: 4 (over z).
Axes of the slice: x: 2, y: 2, z: 4, core: 2. Of those that a mesh axis runs over, the one named last changes fastest.
Arguments:
- hidden: bfloat16 [4, 1024, 2048], P('fsdp', 'seq'), may hold values from -6 to 6
- embedded: bfloat16 [4, 1024, 2048], P('fsdp', 'seq'), may hold values from -6 to 6
- segment: int32 [4, 1024], P('fsdp', 'seq'), may hold values from 0 to 2, as said below
- position: int32 [4, 1024], P('fsdp', 'seq'), may hold values from 0 to 5119, as said below
- attn_gain: bfloat16 [4096], P(('seq', 'fsdp')), may hold values from 0.5 to 1.5
- query_key_value_weight: bfloat16 [3, 4096, 4096], P(None, 'fsdp', 'seq'), may hold values from -0.09375 to 0.09375
- query_key_value_down: bfloat16 [4096, 384], P(('seq', 'fsdp')), may hold values from -0.09375 to 0.09375
- query_key_value_up: bfloat16 [3, 128, 4096], P(None, 'fsdp', 'seq'), may hold values from -0.5 to 0.5
- out_weight: bfloat16 [4096, 2048], P('seq', 'fsdp'), may hold values from -0.375 to 0.375
- mlp_gain: bfloat16 [2048], P(('seq', 'fsdp')), may hold values from 0.5 to 1.5
- gate_up_weight: bfloat16 [2, 2048, 8192], P(None, 'fsdp', 'seq'), may hold values from -0.125 to 0.125
- feedforward_down_weight: bfloat16 [2048, 128], P(('seq', 'fsdp')), may hold values from -0.125 to 0.125
- feedforward_up_weight: bfloat16 [2, 128, 8192], P(None, 'fsdp', 'seq'), may hold values from -0.5 to 0.5
- down_weight: bfloat16 [8192, 2048], P('seq', 'fsdp'), may hold values from -0.125 to 0.125
- scan_gain: bfloat16 [2048], P(('seq', 'fsdp')), may hold values from 0.5 to 1.5
- zx_weight: bfloat16 [2, 2048, 4096], P(None, 'fsdp', 'seq'), may hold values from -0.125 to 0.125
- bc_weight: bfloat16 [2048, 256], P(('seq', 'fsdp')), may hold values from -0.125 to 0.125
- dt_weight: bfloat16 [2048, 64], P('fsdp', 'seq'), may hold values from -0.125 to 0.125
- conv_x: bfloat16 [4, 4096], P(None, ('seq', 'fsdp')), may hold values from -3 to 3
- conv_bc: bfloat16 [4, 256], P(None, ('seq', 'fsdp')), may hold values from -3 to 3
- dt_bias: float32 [64], P('seq'), may hold values from -2 to 0
- decay_rate: float32 [64], P('seq'), may hold values from 0.0003 to 0.1
- skip_gain: float32 [64], P('seq'), may hold values from 0.5 to 1.5
- inner_gain: bfloat16 [4096], P(('seq', 'fsdp')), may hold values from 0.5 to 1.5
- out_proj: bfloat16 [4096, 2048], P('seq', 'fsdp'), may hold values from -0.09375 to 0.09375
- cotangent: bfloat16 [4, 1024, 2048], P('fsdp', 'seq'), may hold values from -6 to 6
Outputs:
- output: bfloat16 [4, 1024, 2048], P('fsdp', 'seq')
- grad_hidden: float32 [4, 1024, 2048], P('fsdp', 'seq')
- grad_embedded: float32 [4, 1024, 2048], P('fsdp', 'seq')
- grad_attn_gain: float32 [4096], P(('seq', 'fsdp'))
- grad_qkv_weight: float32 [3, 4096, 4096], P(None, 'fsdp', 'seq')
- grad_qkv_down: float32 [4096, 384], P(('seq', 'fsdp'))
- grad_qkv_up: float32 [3, 128, 4096], P(None, 'fsdp', 'seq')
- grad_out_weight: float32 [4096, 2048], P('seq', 'fsdp')
- grad_mlp_gain: float32 [2048], P(('seq', 'fsdp'))
- grad_gate_up: float32 [2, 2048, 8192], P(None, 'fsdp', 'seq')
- grad_mlp_down: float32 [2048, 128], P(('seq', 'fsdp'))
- grad_mlp_up: float32 [2, 128, 8192], P(None, 'fsdp', 'seq')
- grad_down_weight: float32 [8192, 2048], P('seq', 'fsdp')
- grad_scan_gain: float32 [2048], P(('seq', 'fsdp'))
- grad_zx_weight: float32 [2, 2048, 4096], P(None, 'fsdp', 'seq')
- grad_bc_weight: float32 [2048, 256], P(('seq', 'fsdp'))
- grad_dt_weight: float32 [2048, 64], P('fsdp', 'seq')
- grad_conv_x: float32 [4, 4096], P(None, ('seq', 'fsdp'))
- grad_conv_bc: float32 [4, 256], P(None, ('seq', 'fsdp'))
- grad_dt_bias: float32 [64], P('seq')
- grad_decay_rate: float32 [64], P('seq')
- grad_skip_gain: float32 [64], P('seq')
- grad_inner_gain: float32 [4096], P(('seq', 'fsdp'))
- grad_out_proj: float32 [4096, 2048], P('seq', 'fsdp')
The draws below stay inside these ranges and needn't reach their ends.
Inputs may be any that keep to these rules, and one draw needn't show every extreme that they name: segment numbers the three documents of a pack 0, 1, 2 in order; the first and the last document each have fewer than 1024 / 8 positions. Within a document the position rises by one from each place to the next; the first document of a pack starts at 0 and the last one ends at 5119.
All inputs are finite; a program needn't handle non-finite values.
Results may differ from the reference program's by a relative error of at most 0.038.
The reference program's roundings to bfloat16 on the way count: a program that leaves them out, or rounds other values in their place, can miss the bound.
Values may be sent and summed in bfloat16 or wider, within the bound.
No kernel may reach another device: no remote copies, remote signals or barrier semaphores. Data moves between devices by JAX's collectives and lax.ppermute only.
A program may use at most 640 MiB of HBM per device.

```python
import math
import jax
import jax.numpy as jnp
from jax import lax

MODEL_WIDTH = 2048
NH = 32
HD = 128
JOINED_WIDTH = 4096
ADAPTER_RANK = 128
FF = 8192
MH = 64
DI = 4096
NS = 128
KC = 4
ROWS = 512
SCAN_BLOCK = 128
SEQLEN = 1024
PACKS = 4
N_SEQ = 8


def pack_bounds(key):
    span = SEQLEN // N_SEQ
    first_end = jax.random.randint(jax.random.fold_in(key, 11), (PACKS, 1), 1, span)
    last_start = SEQLEN - jax.random.randint(jax.random.fold_in(key, 12), (PACKS, 1), 1, span)
    places = jnp.arange(SEQLEN, dtype=jnp.int32)[None, :]
    documents = (places >= first_end).astype(jnp.int32) + (places >= last_start).astype(jnp.int32)
    return (first_end, last_start, places, documents)


def draw_segment(key, part):
    first_end, last_start, places, documents = pack_bounds(key)
    return documents


def draw_position(key, part):
    own_key = jax.random.fold_in(key, 5)
    first_end, last_start, places, documents = pack_bounds(key)
    middle = jax.random.randint(own_key, (PACKS, 1), 0, 4096)
    starts = jnp.where(documents == 0, 0, jnp.where(documents == 1, first_end, last_start))
    offsets = jnp.where(documents == 0, 0, jnp.where(documents == 1, middle, 4096 + last_start))
    return offsets + places - starts


def levels(rng, dims, pieces, smallest, high):
    def one(dim, blocks):
        draws = jax.random.uniform(jax.random.fold_in(jax.random.fold_in(rng, 6), dim), (blocks,), jnp.float32, smallest / len(pieces), high / len(pieces))
        return jnp.repeat(jnp.exp(draws), dims[dim] // blocks).reshape((-1,) + (1,) * (len(dims) - dim - 1))

    factor_of = one(*pieces[0])
    for cut in pieces[1:]:
        factor_of = factor_of * one(*cut)
    return factor_of


def normal_values(stream_key, shape, spread, reach, pieces=(), kind=jnp.bfloat16):
    values = jax.random.normal(stream_key, shape, jnp.float32) * spread
    if len(pieces) > 0:
        values = levels(stream_key, shape, pieces, -0.22, 0.18) * values
    return jnp.clip(values, min=-reach, max=reach).astype(kind)


def setup_inputs(seed: int = 0) -> dict:
    key_of = jax.random.split(jax.random.key(seed), 27)
    return {
        "hidden": normal_values(key_of[0], (PACKS, SEQLEN, MODEL_WIDTH), 1.0, 6.0, ((0, 4), (1, 8))),
        "embedded": normal_values(key_of[1], (PACKS, SEQLEN, MODEL_WIDTH), 1.0, 6.0, ((0, 4), (1, 8))),
        "segment": draw_segment(jax.random.fold_in(key_of[26], 71), 0),
        "position": draw_position(jax.random.fold_in(key_of[26], 71), 0),
        "attn_gain": jnp.clip(1.0 + 0.1 * jax.random.normal(key_of[4], (JOINED_WIDTH,), jnp.float32), 0.5, 1.5).astype(jnp.bfloat16),
        "query_key_value_weight": normal_values(key_of[5], (3, JOINED_WIDTH, JOINED_WIDTH), JOINED_WIDTH ** -0.5, 0.09375, ((1, 4), (2, 8))),
        "query_key_value_down": normal_values(key_of[6], (JOINED_WIDTH, 3 * ADAPTER_RANK), JOINED_WIDTH ** -0.5, 0.09375, ((0, 32),)),
        "query_key_value_up": normal_values(key_of[7], (3, ADAPTER_RANK, JOINED_WIDTH), ADAPTER_RANK ** -0.5, 0.5, ((1, 4), (2, 8))),
        "out_weight": normal_values(key_of[8], (JOINED_WIDTH, MODEL_WIDTH), (JOINED_WIDTH // 16) ** -0.5, 0.375, ((0, 8), (1, 4))),
        "mlp_gain": jnp.clip(1.0 + 0.1 * jax.random.normal(key_of[9], (MODEL_WIDTH,), jnp.float32), 0.5, 1.5).astype(jnp.bfloat16),
        "gate_up_weight": normal_values(key_of[10], (2, MODEL_WIDTH, FF), MODEL_WIDTH ** -0.5, 0.125, ((1, 4), (2, 8))),
        "feedforward_down_weight": normal_values(key_of[11], (MODEL_WIDTH, ADAPTER_RANK), MODEL_WIDTH ** -0.5, 0.125, ((0, 32),)),
        "feedforward_up_weight": normal_values(key_of[12], (2, ADAPTER_RANK, FF), ADAPTER_RANK ** -0.5, 0.5, ((1, 4), (2, 8))),
        "down_weight": normal_values(key_of[13], (FF, MODEL_WIDTH), (FF // 4) ** -0.5, 0.125, ((0, 8), (1, 4))),
        "scan_gain": jnp.clip(1.0 + 0.1 * jax.random.normal(key_of[14], (MODEL_WIDTH,), jnp.float32), 0.5, 1.5).astype(jnp.bfloat16),
        "zx_weight": normal_values(key_of[15], (2, MODEL_WIDTH, DI), MODEL_WIDTH ** -0.5, 0.125, ((1, 4), (2, 8))),
        "bc_weight": normal_values(key_of[16], (MODEL_WIDTH, 2 * NS), MODEL_WIDTH ** -0.5, 0.125, ((0, 32),)),
        "dt_weight": normal_values(key_of[17], (MODEL_WIDTH, MH), MODEL_WIDTH ** -0.5, 0.125, ((0, 4), (1, 8))),
        "conv_x": normal_values(key_of[18], (KC, DI), 0.5, 3.0, ((1, 32),)),
        "conv_bc": normal_values(key_of[19], (KC, 2 * NS), 0.5, 3.0, ((1, 32),)),
        "dt_bias": jnp.clip(-2.0 + 2.0 * jax.random.uniform(key_of[20], (MH,), jnp.float32) ** levels(key_of[20], (MH,), ((0, 8),), -0.2, 0.2), -2.0, 0.0),
        "decay_rate": jnp.clip(jnp.exp(math.log(0.1) - 5.809143 * jax.random.uniform(key_of[21], (MH,), jnp.float32) ** levels(key_of[21], (MH,), ((0, 8),), -0.2, 0.2)), 0.0003, 0.1),
        "skip_gain": jnp.clip(0.5 + 1.0 * jax.random.uniform(key_of[22], (MH,), jnp.float32) ** levels(key_of[22], (MH,), ((0, 8),), -0.2, 0.2), 0.5, 1.5),
        "inner_gain": jnp.clip(1.0 + 0.1 * jax.random.normal(key_of[23], (DI,), jnp.float32), 0.5, 1.5).astype(jnp.bfloat16),
        "out_proj": normal_values(key_of[24], (DI, MODEL_WIDTH), DI ** -0.5, 0.09375, ((0, 8), (1, 4))),
        "cotangent": normal_values(key_of[25], (PACKS, SEQLEN, MODEL_WIDTH), 1.0, 6.0, ((0, 4), (1, 8))),
    }


@jax.custom_vjp
def lowered_value(v):
    return lax.optimization_barrier(v.astype(jnp.bfloat16)).astype(jnp.float32)

@jax.custom_vjp
def lowered_backward(v):
    return v

def low_keep(v):
    return (lowered_value(v), None)

def low_pass(kept, grad):
    return (grad,)

def back_keep(v):
    return (v, None)

def back_low(kept, grad):
    return (lowered_value(grad),)
lowered_value.defvjp(low_keep, low_pass)
lowered_backward.defvjp(back_keep, back_low)
epsilon = 1e-06
highest = lax.Precision.HIGHEST

def product_result(left, right):
    return jnp.dot(left, right, precision=highest)

def rms_norm(values, gain):
    return values * lax.rsqrt(lax.optimization_barrier(jnp.mean(values * values, axis=-1, keepdims=True)) + epsilon) * gain

def gelu_gate(gate_values, upper_value):
    return jax.nn.gelu(gate_values) * upper_value

def rotate(values, places, turn):
    half_size = values.shape[-1] // 2
    frequency = jnp.exp(jnp.arange(half_size, dtype=jnp.float32) * (-2.0 * math.log(10000.0) / values.shape[-1]))
    angles = places.astype(jnp.float32)[:, None] * frequency[None, :]
    cosine = jnp.cos(angles)[:, None, :]
    sine = turn * jnp.sin(angles)[:, None, :]
    first_half = values[..., :half_size]
    second_half = values[..., half_size:]
    return jnp.concatenate([first_half * cosine - second_half * sine, second_half * cosine + first_half * sine], axis=-1)

def conv_mix(values, taps, segment_ids):
    result = values * taps[0]
    for shift_by in range(1, taps.shape[0]):
        moved = jnp.pad(values, ((shift_by, 0), (0, 0)))[:-shift_by]
        earlier = jnp.pad(segment_ids, (shift_by, 0), constant_values=-1)[:-shift_by]
        result = result + jnp.where((earlier == segment_ids)[:, None], moved, 0.0) * taps[shift_by]
    return result

def scan_blocks(values, steps, rate, in_state, out_state, segment_ids):
    length, heads, size = values.shape
    states = in_state.shape[1]
    count = length // SCAN_BLOCK
    places = jnp.arange(SCAN_BLOCK, dtype=jnp.int32)

    def block_step(carry, block):
        state, last_seg = carry
        block_values, block_steps, block_in, block_out, block_seg = block
        running = jnp.cumsum(-block_steps * rate[None, :], axis=0)
        allowed = (places[None, :] <= places[:, None]) & (block_seg[None, :] == block_seg[:, None])
        spread_log = running[:, None, :] - running[None, :, :]
        decay = jnp.where(allowed[:, :, None], jnp.exp(jnp.minimum(spread_log, 0.0)), 0.0)
        inner = jnp.dot(block_out, block_in.T, precision=highest)
        weights = decay * inner[:, :, None] * block_steps[None, :, :]
        local = jnp.einsum('tsm,smp->tmp', weights, block_values, precision=highest)
        carried = jnp.einsum('tn,mpn->tmp', block_out, state, precision=highest)
        entering = jnp.exp(running) * (block_seg == last_seg).astype(jnp.float32)[:, None]
        carried = carried * entering[:, :, None]
        leaving = jnp.exp(running[-1][None, :] - running) * block_steps * (block_seg == block_seg[-1]).astype(jnp.float32)[:, None]
        kept = jnp.exp(running[-1]) * (block_seg[-1] == last_seg).astype(jnp.float32)
        state = state * kept[:, None, None] + jnp.einsum('sm,smp,sn->mpn', leaving, block_values, block_in, precision=highest)
        return ((state, block_seg[-1]), local + carried)
    blocks = (values.reshape(count, SCAN_BLOCK, heads, size), steps.reshape(count, SCAN_BLOCK, heads), in_state.reshape(count, SCAN_BLOCK, states), out_state.reshape(count, SCAN_BLOCK, states), segment_ids.reshape(count, SCAN_BLOCK))
    start = (jnp.zeros((heads, size, states), jnp.float32), jnp.array(-1, jnp.int32))
    ignored, mixed = lax.scan(jax.checkpoint(block_step), start, blocks)
    return mixed.reshape(length, heads, size)

def scan_core(z_part, x_part, step_part, bc_part, conv_local, conv_common, bias, rate, skip, segment_ids):
    length = x_part.shape[0]
    heads = bias.shape[0]
    size = x_part.shape[1] // heads
    states = bc_part.shape[1] // 2
    x_conv = jax.nn.silu(conv_mix(x_part, conv_local, segment_ids))
    bc_conv = jax.nn.silu(conv_mix(bc_part, conv_common, segment_ids))
    steps = jax.nn.softplus(step_part + bias[None, :])
    values = x_conv.reshape(length, heads, size)
    mixed = scan_blocks(values, steps, rate, bc_conv[:, :states], bc_conv[:, states:], segment_ids)
    mixed = mixed + skip[None, :, None] * values
    return mixed.reshape(length, heads * size) * jax.nn.silu(z_part)

def attention(query, key_rows, value_rows, segment_ids):
    length = query.shape[0]
    scale = query.shape[-1] ** (-0.5)
    count = length // ROWS
    columns = jnp.arange(length, dtype=jnp.int32)

    def score_rows(block_index):
        start = block_index * ROWS
        query_rows = lax.dynamic_slice_in_dim(query, start, ROWS, 0)
        row_ids = start + jnp.arange(ROWS, dtype=jnp.int32)
        row_seg = lax.dynamic_slice_in_dim(segment_ids, start, ROWS, 0)
        scores = lowered_backward(jnp.einsum('qhd,khd->hqk', query_rows, key_rows, precision=highest)) * scale
        allowed = (columns[None, :] <= row_ids[:, None]) & (segment_ids[None, :] == row_seg[:, None])
        scores = jnp.where(allowed[None], scores, -1e+30)
        probs = jnp.exp(scores - lax.optimization_barrier(jnp.max(scores, axis=2, keepdims=True)))
        probs = probs / lax.optimization_barrier(jnp.sum(probs, axis=2, keepdims=True))
        return jnp.einsum('hqk,khd->qhd', lowered_value(probs), value_rows, precision=highest)
    blocks = lax.map(jax.checkpoint(score_rows), jnp.arange(count, dtype=jnp.int32))
    return blocks.reshape(length, query.shape[1], query.shape[2])

def layer(hidden_rows, embedded_rows, segment_ids, places, attn_gain, query_key_value_weight, query_key_value_down, query_key_value_up, out_weight, mlp_gain, gate_up_weight, feedforward_down_weight, feedforward_up_weight, down_weight, scan_gain, zx_weight, bc_weight, dt_weight, conv_x, conv_bc, dt_bias, decay_rate, skip_gain, inner_gain, out_proj):
    length = hidden_rows.shape[0]
    joined = jnp.concatenate([hidden_rows, embedded_rows], axis=1)
    normalized_input = lowered_value(rms_norm(joined, attn_gain))
    adapter_row_set = lowered_value(lowered_backward(product_result(normalized_input, query_key_value_down)))
    projected = []
    for part in range(3):
        summed_total = product_result(normalized_input, query_key_value_weight[part]) + product_result(adapter_row_set[:, part * ADAPTER_RANK:(part + 1) * ADAPTER_RANK], query_key_value_up[part])
        projected.append(lowered_backward(summed_total).reshape(length, NH, HD))
    query = lowered_value(rotate(projected[0], places, 1.0))
    key_rows = lowered_value(rotate(projected[1], places, 1.0))
    value_rows = lowered_value(projected[2])
    mixed = lowered_value(lowered_backward(attention(query, key_rows, value_rows, segment_ids))).reshape(length, JOINED_WIDTH)
    first = hidden_rows + lowered_backward(product_result(mixed, out_weight))
    feedforward_input = lowered_value(rms_norm(first, mlp_gain))
    feedforward_adapter = lowered_value(lowered_backward(product_result(feedforward_input, feedforward_down_weight)))
    gate_values = lowered_backward(product_result(feedforward_input, gate_up_weight[0]) + product_result(feedforward_adapter, feedforward_up_weight[0]))
    upper_value = lowered_backward(product_result(feedforward_input, gate_up_weight[1]) + product_result(feedforward_adapter, feedforward_up_weight[1]))
    activated = lowered_value(gelu_gate(gate_values, upper_value))
    second = first + lowered_backward(product_result(activated, down_weight))
    scan_in = lowered_value(rms_norm(second, scan_gain))
    bc_rows = lowered_value(lowered_backward(product_result(scan_in, bc_weight)))
    z_part = lowered_backward(product_result(scan_in, zx_weight[0]))
    x_part = lowered_backward(product_result(scan_in, zx_weight[1]))
    step_part = lowered_backward(product_result(scan_in, dt_weight))
    gated = scan_core(z_part, x_part, step_part, bc_rows, conv_x, conv_bc, dt_bias, decay_rate, skip_gain, segment_ids)
    scan_norm = lowered_value(rms_norm(gated, inner_gain))
    return second + lowered_backward(product_result(scan_norm, out_proj))

def reference(hidden, embedded, segment, position, attn_gain, query_key_value_weight, query_key_value_down, query_key_value_up, out_weight, mlp_gain, gate_up_weight, feedforward_down_weight, feedforward_up_weight, down_weight, scan_gain, zx_weight, bc_weight, dt_weight, conv_x, conv_bc, dt_bias, decay_rate, skip_gain, inner_gain, out_proj, cotangent):
    weights = [item.astype(jnp.float32) for item in (attn_gain, query_key_value_weight, query_key_value_down, query_key_value_up, out_weight, mlp_gain, gate_up_weight, feedforward_down_weight, feedforward_up_weight, down_weight, scan_gain, zx_weight, bc_weight, dt_weight, conv_x, conv_bc, dt_bias, decay_rate, skip_gain, inner_gain, out_proj)]

    def pack_step(totals, pack):
        hidden_rows, embedded_rows, segment_ids, places, cot_rows = pack

        def forward(hidden_in, embedded_in, *params):
            return layer(hidden_in, embedded_in, segment_ids, places, *params)
        result, pull = jax.vjp(forward, hidden_rows, embedded_rows, *weights)
        grads = pull(cot_rows)
        totals = [total + grad for total, grad in zip(totals, grads[2:])]
        return (totals, (result.astype(jnp.bfloat16), grads[0], grads[1]))
    zeros = [jnp.zeros_like(item) for item in weights]
    totals, stacked = lax.scan(pack_step, zeros, (hidden.astype(jnp.float32), embedded.astype(jnp.float32), segment, position, cotangent.astype(jnp.float32)))
    output, grad_hidden, grad_embedded = stacked
    g_attn_gain, g_qkv_weight, g_qkv_down, g_qkv_up, g_out_weight, g_mlp_gain, g_gate_up, g_mlp_down, g_mlp_up, g_down_weight, g_scan_gain, g_zx_weight, g_bc_weight, g_dt_weight, g_conv_x, g_conv_bc, g_dt_bias, g_decay_rate, g_skip_gain, g_inner_gain, g_out_proj = totals
    return (output, grad_hidden, grad_embedded, g_attn_gain, g_qkv_weight, g_qkv_down, g_qkv_up, g_out_weight, g_mlp_gain, g_gate_up, g_mlp_down, g_mlp_up, g_down_weight, g_scan_gain, g_zx_weight, g_bc_weight, g_dt_weight, g_conv_x, g_conv_bc, g_dt_bias, g_decay_rate, g_skip_gain, g_inner_gain, g_out_proj)
```

```python
import functools
import math

import jax
import jax.numpy as jnp
from jax import lax
from jax.experimental import pallas as pl
from jax.experimental.pallas import tpu as pltpu
from jax.sharding import PartitionSpec as P

MODEL_WIDTH = 2048
ADAPTER_RANK = 128
DI = 4096
epsilon = 1e-06

f32 = jnp.float32
bf16 = jnp.bfloat16
T = 128
HS = 64
VMEM = 48 * 1024 * 1024


def dot(a, b, ca, cb):
    return lax.dot_general(
        a.astype(bf16), b.astype(bf16), (((ca,), (cb,)), ((), ())), preferred_element_type=f32
    )


def masked_sum(mask, values):
    high = values.astype(bf16)
    rest = values - high.astype(f32)
    middle = rest.astype(bf16)
    low = (rest - middle.astype(f32)).astype(bf16)
    wide = mask.astype(bf16)
    return dot(
        jnp.concatenate([wide, wide, wide], axis=1),
        jnp.concatenate([high, middle, low], axis=0),
        1,
        0,
    )


def sigmoid(v):
    return 1.0 / (1.0 + jnp.exp(-v))


def iota(shape, dim):
    return lax.broadcasted_iota(jnp.int32, shape, dim)


def spread_heads(per_head, width):
    rows = per_head.shape[0]
    low = iota((rows, 2 * HS), 1) < HS
    return jnp.concatenate(
        [
            jnp.where(low, per_head[:, 2 * j : 2 * j + 1], per_head[:, 2 * j + 1 : 2 * j + 2])
            for j in range(width // (2 * HS))
        ],
        axis=1,
    )


def sum_heads(values):
    width = values.shape[1]
    member = (iota((width, 128), 0) // HS == iota((width, 128), 1)).astype(bf16)
    high = values.astype(bf16)
    low = (values - high.astype(f32)).astype(bf16)
    return dot(high, member, 1, 0) + dot(low, member, 1, 0)


def shift_down(values, tail, by):
    moved = pltpu.roll(values, by, 0)
    first = jnp.where(iota(tail.shape, 0) < by, pltpu.roll(tail, by, 0), moved[:8])
    return jnp.concatenate([first, moved[8:]], axis=0)


def shift_up(values, head, by):
    size = values.shape[0]
    moved = pltpu.roll(values, size - by, 0)
    last = jnp.where(iota(head.shape, 0) >= 8 - by, pltpu.roll(head, 8 - by, 0), moved[size - 8 :])
    return jnp.concatenate([moved[: size - 8], last], axis=0)


def conv(values, tail, taps, marks):
    result = values * taps[0:1]
    for k in range(1, 4):
        result = result + shift_down(values, tail, k) * marks[:, k - 1 : k] * taps[k : k + 1]
    return result


def block_terms(steps_raw, marks, seg_row, bias, rate):
    steps = steps_raw + bias
    steps = jnp.maximum(steps, 0.0) + jnp.log1p(jnp.exp(-jnp.abs(steps)))
    lower = iota((T, T), 1) <= iota((T, T), 0)
    running = masked_sum(lower, -steps * rate)
    allowed = lower & (marks[:, 6:7] == seg_row)
    entering = jnp.exp(running) * marks[:, 3:4]
    ending = jnp.exp(running[T - 1 : T] - running) * marks[:, 4:5]
    kept = jnp.exp(running[T - 1 : T]) * marks[T - 1 : T, 5:6]
    return steps, running, allowed, entering, ending, kept


def decay_of(running, running_t, allowed, m):
    spread = running[:, m : m + 1] - running_t[m : m + 1, :]
    return jnp.where(allowed, jnp.exp(jnp.minimum(spread, 0.0)), 0.0)


def scan_forward_kernel(
    order, x_ref, step_ref, bc_ref, mark_ref, seg_ref, tapx_ref, tapbc_ref, head_ref,
    y_ref, states_ref, state, tail_x, tail_bc,
):
    block = pl.program_id(0)

    @pl.when(block == 0)
    def _():
        state[...] = jnp.zeros_like(state)
        tail_x[...] = jnp.zeros_like(tail_x)
        tail_bc[...] = jnp.zeros_like(tail_bc)

    width = x_ref.shape[1]
    marks = mark_ref[...]
    x = x_ref[...]
    xs = conv(x, tail_x[...], tapx_ref[...], marks)
    xs = xs * sigmoid(xs)
    tail_x[...] = x[T - 8 :]
    bc = bc_ref[...]
    bcs = conv(bc, tail_bc[...], tapbc_ref[...], marks)
    bcs = bcs * sigmoid(bcs)
    tail_bc[...] = bc[T - 8 :]
    b_rows, c_rows = bcs[:, :128], bcs[:, 128:]
    bias, rate, skip = head_ref[0:1], head_ref[1:2], head_ref[2:3]
    steps, running, allowed, entering, ending, kept = block_terms(
        step_ref[...], marks, seg_ref[0], bias, rate
    )
    running_t, steps_t = running.T, steps.T
    inner = dot(c_rows, b_rows, 1, 1)
    held = state[...]
    states_ref[0] = held
    carried = dot(c_rows, held, 1, 0)
    low = iota((T, 2 * HS), 1) < HS
    parts = []
    for j in range(width // (2 * HS)):
        pair = xs[:, 2 * HS * j : 2 * HS * (j + 1)].astype(bf16)
        made = [
            dot(decay_of(running, running_t, allowed, m) * inner * steps_t[m : m + 1], pair, 1, 0)
            for m in (2 * j, 2 * j + 1)
        ]
        parts.append(jnp.where(low, made[0], made[1]))
    local = jnp.concatenate(parts, axis=1)
    y_ref[...] = local + carried * spread_heads(entering, width) + xs * spread_heads(skip, width)
    leaving = spread_heads(ending * steps, width) * xs
    state[...] = held * spread_heads(kept, width) + dot(b_rows, leaving, 0, 0)


def scan_backward_kernel(
    order, x_ref, xt_ref, z_ref, step_ref, bc_ref, bct_ref, mark_ref, seg_ref, tapx_ref, tapbc_ref,
    head_ref, y_ref, states_ref, gn_ref, row_ref, inner_ref,
    gzx_ref, gside_ref, gtapx_ref, gtapbc_ref, ghead_ref, ginner_ref,
    d_state, cols, next_x, next_bc,
):
    @pl.when(pl.program_id(0) == 0)
    def _():
        for ref in (d_state, cols, next_x, next_bc, gtapx_ref, gtapbc_ref, ghead_ref, ginner_ref):
            ref[...] = jnp.zeros_like(ref)

    width = x_ref.shape[1]
    marks = mark_ref[...]
    tapx, tapbc = tapx_ref[...], tapbc_ref[...]
    x, tail_x = x_ref[...], xt_ref[...]
    xc = conv(x, tail_x, tapx, marks)
    xsig = sigmoid(xc)
    xs = xc * xsig
    bc, tail_bc = bc_ref[...], bct_ref[...]
    bcc = conv(bc, tail_bc, tapbc, marks)
    bcsig = sigmoid(bcc)
    bcs = bcc * bcsig
    b_rows, c_rows = bcs[:, :128].astype(bf16), bcs[:, 128:].astype(bf16)
    bias, rate, skip = head_ref[0:1], head_ref[1:2], head_ref[2:3]
    steps, running, allowed, entering, ending, kept = block_terms(
        step_ref[...], marks, seg_ref[0], bias, rate
    )
    running_t, steps_t = running.T, steps.T

    z, y, gn = z_ref[...], y_ref[...], gn_ref[...]
    row_terms = row_ref[...].T
    inv, cross = row_terms[:, 0:1], row_terms[:, 1:2]
    zsig = sigmoid(z)
    zs = z * zsig
    gated = y * zs
    ginner_ref[...] += jnp.sum(gn * gated * inv, axis=0, keepdims=True)
    g_gated = gn * inner_ref[...] * inv - gated * cross
    gzx_ref[:, :width] = (g_gated * y * (zsig + zs * (1.0 - zsig))).astype(bf16)
    dy = g_gated * zs

    inner = dot(c_rows, b_rows, 1, 1)
    held = states_ref[0]
    held_low = held.astype(bf16)
    ds = d_state[...]
    ds_low = ds.astype(bf16)
    entering_wide = spread_heads(entering, width)
    leaving_wide = spread_heads(ending * steps, width)
    kept_wide = spread_heads(kept, width)

    low = iota((T, 2 * HS), 1) < HS
    lane = iota((T, 128), 1)
    d_inner = jnp.zeros((T, T), f32)
    rows = jnp.zeros((T, 128), f32)
    parts = []
    for j in range(width // (2 * HS)):
        cut = slice(2 * HS * j, 2 * HS * (j + 1))
        x_pair = xs[:, cut].astype(bf16)
        dy_pair = dy[:, cut]
        dy_low = dy_pair.astype(bf16)
        made = []
        for m in (2 * j, 2 * j + 1):
            mine = low if m % 2 == 0 else ~low
            decay = decay_of(running, running_t, allowed, m)
            grown = decay * steps_t[m : m + 1]
            d_weight = dot(jnp.where(mine, dy_pair, 0.0), x_pair, 1, 1)
            d_inner = d_inner + d_weight * grown
            pushed = d_weight * decay * inner
            cols[m : m + 1, :] = jnp.sum(pushed, axis=0, keepdims=True)
            rows = rows + jnp.where(
                lane == m, jnp.sum(pushed * steps_t[m : m + 1], axis=1, keepdims=True), 0.0
            )
            made.append(dot(grown * inner, dy_low, 0, 0))
        parts.append(jnp.where(low, made[0], made[1]))
    v_rows = dot(b_rows, ds_low, 1, 0)
    dxs = jnp.concatenate(parts, axis=1) + dy * spread_heads(skip, width) + leaving_wide * v_rows
    u_rows = (dy * entering_wide).astype(bf16)
    carried = dot(c_rows, held_low, 1, 0)
    d_c = dot(d_inner, b_rows, 1, 0) + dot(u_rows, held_low, 1, 1)
    d_b = dot(d_inner, c_rows, 0, 0) + dot(leaving_wide * xs, ds_low, 1, 1)
    d_step = cols[...].T
    d_running = rows - d_step * steps
    d_running = d_running + sum_heads(dy * carried) * entering
    d_ending = sum_heads(v_rows * xs)
    d_step = d_step + d_ending * ending
    moved = d_ending * ending * steps
    d_kept = sum_heads(jnp.broadcast_to(jnp.sum(ds * held, axis=0, keepdims=True), (8, width)))
    last = jnp.sum(moved, axis=0, keepdims=True) + d_kept[0:1] * kept
    d_running = d_running - moved + jnp.where(iota((T, 128), 0) == T - 1, last, 0.0)
    d_log = masked_sum(iota((T, T), 1) >= iota((T, T), 0), d_running)
    d_step = d_step - rate * d_log
    d_raw = d_step * sigmoid(step_ref[...] + bias)
    gside_ref[:, :128] = d_raw.astype(bf16)
    d_skip = sum_heads(
        jnp.broadcast_to(jnp.sum(dy * xs, axis=0, keepdims=True), (8, width))
    )
    ghead_ref[0:1] += jnp.sum(d_raw, axis=0, keepdims=True)
    ghead_ref[1:2] -= jnp.sum(steps * d_log, axis=0, keepdims=True)
    ghead_ref[2:3] += d_skip[0:1]
    d_state[...] = ds * kept_wide + dot(c_rows, u_rows, 0, 0)

    def conv_back(grad, values, tail, taps, following, gtap_ref):
        result = grad * taps[0:1]
        gtap_ref[0:1] += jnp.sum(grad * values, axis=0, keepdims=True)
        for k in range(1, 4):
            marked = grad * marks[:, k - 1 : k]
            gtap_ref[k : k + 1] += jnp.sum(
                marked * shift_down(values, tail, k), axis=0, keepdims=True
            )
            sent = marked * taps[k : k + 1]
            result = result + shift_up(sent, following[k - 1], k)
            following[k - 1] = sent[:8]
        return result

    dxc = dxs * (xsig + xs * (1.0 - xsig))
    gzx_ref[:, width:] = conv_back(dxc, x, tail_x, tapx, next_x, gtapx_ref).astype(bf16)
    dbc = jnp.concatenate([d_b, d_c], axis=1) * (bcsig + bcs * (1.0 - bcsig))
    gside_ref[:, 128:] = conv_back(dbc, bc, tail_bc, tapbc, next_bc, gtapbc_ref).astype(bf16)


def scan_marks(seg):
    length = seg.shape[0]
    blocks = seg.reshape(-1, T)
    last = jnp.concatenate([jnp.full((1,), -1, seg.dtype), blocks[:-1, -1]])
    cols = []
    for k in range(1, 4):
        earlier = jnp.pad(seg, (k, 0), constant_values=-1)[:-k]
        cols.append(earlier == seg)
    cols.append((blocks == last[:, None]).reshape(length))
    cols.append((blocks == blocks[:, -1:]).reshape(length))
    cols.append(jnp.repeat(blocks[:, -1] == last, T))
    cols.append(seg)
    cols.append(seg)
    marks = jnp.stack([c.astype(f32) for c in cols], axis=1)
    return marks, blocks.astype(f32)[:, None, :]


def whole(shape):
    return pl.BlockSpec(shape, lambda *_: (0,) * len(shape))


def scan_forward(order, zx, step, bc, marks, seg_rows, tapx, tapbc, heads):
    length, width = zx.shape[0], zx.shape[1] // 2
    count = length // T

    def rows(cols, at=0):
        return pl.BlockSpec((T, cols), lambda i, order: (order[i], at))

    return pl.pallas_call(
        scan_forward_kernel,
        grid_spec=pltpu.PrefetchScalarGridSpec(
            num_scalar_prefetch=1,
            grid=(count,),
            in_specs=[
                rows(width, 1), rows(128), rows(256),
                pl.BlockSpec((T, 8), lambda i, order: (i, 0)),
                pl.BlockSpec((1, 1, T), lambda i, order: (i, 0, 0)),
                whole(tapx.shape), whole(tapbc.shape), whole(heads.shape),
            ],
            out_specs=[rows(width), pl.BlockSpec((1, 128, width), lambda i, order: (i, 0, 0))],
            scratch_shapes=[
                pltpu.VMEM((128, width), f32), pltpu.VMEM((8, width), f32), pltpu.VMEM((8, 256), f32),
            ],
        ),
        out_shape=[
            jax.ShapeDtypeStruct((length, width), f32),
            jax.ShapeDtypeStruct((count, 128, width), f32),
        ],
        compiler_params=pltpu.CompilerParams(vmem_limit_bytes=VMEM),
        cost_estimate=pl.CostEstimate(
            flops=length * width * 128 * 8, bytes_accessed=length * width * 16, transcendentals=length * width * 3
        ),
        name="scan_forward",
    )(order, zx, step, bc, marks, seg_rows, tapx, tapbc, heads)


def scan_backward(
    order, zx, step, bc, marks, seg_rows, tapx, tapbc, heads, y, states, gn, row_terms, inner
):
    length, width = zx.shape[0], zx.shape[1] // 2
    count = length // T

    def rows(cols, at=0):
        return pl.BlockSpec((T, cols), lambda i, order: (order[count - 1 - i], at))

    def tails(cols, at=0):
        return pl.BlockSpec(
            (8, cols),
            lambda i, order: (order[jnp.maximum(count - 2 - i, 0)] * (T // 8) + (T // 8 - 1), at),
        )

    return pl.pallas_call(
        scan_backward_kernel,
        grid_spec=pltpu.PrefetchScalarGridSpec(
            num_scalar_prefetch=1,
            grid=(count,),
            in_specs=[
                rows(width, 1), tails(width, 1), rows(width), rows(128), rows(256), tails(256),
                pl.BlockSpec((T, 8), lambda i, order: (count - 1 - i, 0)),
                pl.BlockSpec((1, 1, T), lambda i, order: (count - 1 - i, 0, 0)),
                whole(tapx.shape), whole(tapbc.shape), whole(heads.shape),
                rows(width),
                pl.BlockSpec((1, 128, width), lambda i, order: (count - 1 - i, 0, 0)),
                rows(width),
                pl.BlockSpec((8, T), lambda i, order: (0, order[count - 1 - i])),
                whole(inner.shape),
            ],
            out_specs=[
                rows(2 * width), rows(384),
                whole((8, width)), whole((8, 256)), whole((8, 128)), whole((1, width)),
            ],
            scratch_shapes=[
                pltpu.VMEM((128, width), f32), pltpu.VMEM((128, T), f32),
                pltpu.VMEM((3, 8, width), f32), pltpu.VMEM((3, 8, 256), f32),
            ],
        ),
        out_shape=[
            jax.ShapeDtypeStruct((length, 2 * width), bf16),
            jax.ShapeDtypeStruct((length, 384), bf16),
            jax.ShapeDtypeStruct((8, width), f32),
            jax.ShapeDtypeStruct((8, 256), f32),
            jax.ShapeDtypeStruct((8, 128), f32),
            jax.ShapeDtypeStruct((1, width), f32),
        ],
        compiler_params=pltpu.CompilerParams(vmem_limit_bytes=VMEM),
        cost_estimate=pl.CostEstimate(
            flops=length * width * 128 * 20, bytes_accessed=length * width * 32, transcendentals=length * width * 3
        ),
        name="scan_backward",
    )(order, zx, zx, zx, step, bc, bc, marks, seg_rows, tapx, tapbc, heads, y, states, gn, row_terms, inner)


BQ = 256


def attention_forward_kernel(
    q_ref, k_ref, v_ref, cos_ref, sin_ref, row_ref, col_ref,
    qr_ref, kr_ref, vr_ref, mixed_ref, lse_ref, bias,
):
    i, h = pl.program_id(0), pl.program_id(1)
    rows = q_ref.shape[0]
    lanes = pl.ds(pl.multiple_of(h * 128, 128), 128)

    def turn(values, cosine, sine):
        return values * cosine + pltpu.roll(values, 64, 1) * sine

    @pl.when(h == 0)
    def _():
        allowed = (col_ref[0:1] <= row_ref[:, 0:1]) & (col_ref[1:2] == row_ref[:, 1:2])
        bias[...] = jnp.where(allowed, 0.0, -1e30)

    @pl.when(i == 0)
    def _():
        kr_ref[:, lanes] = turn(k_ref[...], cos_ref[...], sin_ref[...]).astype(bf16)
        vr_ref[:, lanes] = v_ref[...].astype(bf16)

    here = pl.ds(pl.multiple_of(i * rows, rows), rows)
    q = turn(q_ref[...], cos_ref[here, :], sin_ref[here, :]).astype(bf16)
    qr_ref[...] = q
    scores = dot(q, kr_ref[:, lanes], 1, 1) * (128 ** -0.5) + bias[...]
    largest = jnp.max(scores, axis=1, keepdims=True)
    terms = jnp.exp(scores - largest)
    total = jnp.sum(terms, axis=1, keepdims=True)
    probs = (terms * (1.0 / total)).astype(bf16)
    mixed_ref[...] = dot(probs, vr_ref[:, lanes], 1, 0)
    lse = largest + jnp.log(total)
    lse_ref[...] = jnp.where(iota((rows, 128), 1) == h, lse, lse_ref[...])


def attention_backward_kernel(
    q_ref, k_ref, v_ref, do_ref, mixed_ref, lse_ref, cos_ref, sin_ref, row_ref, col_ref,
    out_ref, bias, dk, dv,
):
    i, h = pl.program_id(0), pl.program_id(1)
    rows = q_ref.shape[0]
    heads = pl.num_programs(1)
    lanes, k_lanes, v_lanes = (
        pl.ds(pl.multiple_of((part * heads + h) * 128, 128), 128) for part in range(3)
    )

    @pl.when(h == 0)
    def _():
        allowed = (col_ref[0:1] <= row_ref[:, 0:1]) & (col_ref[1:2] == row_ref[:, 1:2])
        bias[...] = jnp.where(allowed, 0.0, -1e30)

    @pl.when(i == 0)
    def _():
        dk[:, lanes] = jnp.zeros((dk.shape[0], 128), f32)
        dv[:, lanes] = jnp.zeros((dv.shape[0], 128), f32)

    def turn_back(values, cosine, sine):
        return values * cosine - pltpu.roll(values, 64, 1) * sine

    q, k, v, do = q_ref[...], k_ref[...], v_ref[...], do_ref[...]
    lse = jnp.sum(jnp.where(iota((rows, 128), 1) == h, lse_ref[...], 0.0), axis=1, keepdims=True)
    delta = jnp.sum(do.astype(f32) * mixed_ref[...], axis=1, keepdims=True)
    scale = 128 ** -0.5
    scores = dot(q, k, 1, 1) * scale + bias[...]
    probs = jnp.exp(scores - lse)
    d_probs = dot(do, v, 1, 1)
    d_scores = (probs * (d_probs - delta) * scale).astype(bf16)
    dv[:, lanes] += dot(probs, do, 0, 0)
    dk[:, lanes] += dot(d_scores, q, 0, 0)
    here = pl.ds(pl.multiple_of(i * rows, rows), rows)
    d_query = dot(d_scores, k, 1, 0)
    out_ref[here, lanes] = turn_back(d_query, cos_ref[here, :], sin_ref[here, :]).astype(bf16)

    @pl.when(i == pl.num_programs(0) - 1)
    def _():
        out_ref[:, k_lanes] = turn_back(dk[:, lanes], cos_ref[...], sin_ref[...]).astype(bf16)
        out_ref[:, v_lanes] = dv[:, lanes].astype(bf16)


def rope_tables(places):
    frequency = jnp.exp(
        jnp.arange(64, dtype=f32) * (-2.0 * 9.210340371976184 / 128)
    )
    angles = places.astype(f32)[:, None] * frequency[None, :]
    cosine, sine = jnp.cos(angles), jnp.sin(angles)
    return jnp.concatenate([cosine, cosine], axis=1), jnp.concatenate([-sine, sine], axis=1)


def attention_forward(projected, cosine, sine, row_info, col_info):
    length, width = projected.shape[0], projected.shape[1] // 3
    heads, size = width // 128, min(BQ, length)
    count = length // size
    tile = pl.BlockSpec((size, 128), lambda i, h: (i, h))

    def first(part):
        return pl.BlockSpec(
            (length, 128), lambda i, h: (0, part * heads + jnp.where(i == 0, h, heads - 1))
        )

    return pl.pallas_call(
        attention_forward_kernel,
        grid=(count, heads),
        in_specs=[
            tile, first(1), first(2), whole(cosine.shape), whole(sine.shape),
            pl.BlockSpec((size, 2), lambda i, h: (i, 0)), whole(col_info.shape),
        ],
        out_specs=[
            tile, whole((length, width)), whole((length, width)), tile,
            pl.BlockSpec((size, 128), lambda i, h: (i, 0)),
        ],
        out_shape=[
            jax.ShapeDtypeStruct((length, width), bf16),
            jax.ShapeDtypeStruct((length, width), bf16),
            jax.ShapeDtypeStruct((length, width), bf16),
            jax.ShapeDtypeStruct((length, width), f32),
            jax.ShapeDtypeStruct((length, 128), f32),
        ],
        scratch_shapes=[pltpu.VMEM((size, length), f32)],
        compiler_params=pltpu.CompilerParams(vmem_limit_bytes=VMEM),
        cost_estimate=pl.CostEstimate(
            flops=4 * length * length * width, bytes_accessed=length * width * 22, transcendentals=heads * length * length
        ),
        name="attention_forward",
    )(projected, projected, projected, cosine, sine, row_info, col_info)


def attention_backward(q, k, v, do, mixed, lse, cosine, sine, row_info, col_info):
    length, width = q.shape
    heads, size = width // 128, min(BQ, length)
    count = length // size
    tile = pl.BlockSpec((size, 128), lambda i, h: (i, h))
    full = pl.BlockSpec((length, 128), lambda i, h: (0, h))
    return pl.pallas_call(
        attention_backward_kernel,
        grid=(count, heads),
        in_specs=[
            tile, full, full, tile, tile, pl.BlockSpec((size, 128), lambda i, h: (i, 0)),
            whole(cosine.shape), whole(sine.shape),
            pl.BlockSpec((size, 2), lambda i, h: (i, 0)), whole(col_info.shape),
        ],
        out_specs=whole((length, 3 * width)),
        out_shape=jax.ShapeDtypeStruct((length, 3 * width), bf16),
        scratch_shapes=[
            pltpu.VMEM((size, length), f32), pltpu.VMEM((length, width), f32), pltpu.VMEM((length, width), f32),
        ],
        compiler_params=pltpu.CompilerParams(vmem_limit_bytes=VMEM),
        cost_estimate=pl.CostEstimate(
            flops=10 * length * length * width, bytes_accessed=length * width * 16, transcendentals=heads * length * length
        ),
        name="attention_backward",
    )(q, k, v, do, mixed, lse, cosine, sine, row_info, col_info)


def gelu_backward_kernel(gu_ref, da_ref, out_ref):
    width = da_ref.shape[1]
    gate, upper, da = gu_ref[:, :width], gu_ref[:, width:], da_ref[...]
    factor = math.sqrt(2.0 / math.pi)
    bent = jnp.tanh(factor * (gate + 0.044715 * gate * gate * gate))
    slope = 0.5 * (1.0 + bent) + 0.5 * gate * (1.0 - bent * bent) * factor * (
        1.0 + 3.0 * 0.044715 * gate * gate
    )
    out_ref[:, :width] = (da * upper * slope).astype(bf16)
    out_ref[:, width:] = (da * 0.5 * gate * (1.0 + bent)).astype(bf16)


def gelu_backward(gu, da):
    length, width = da.shape
    rows = 128
    return pl.pallas_call(
        gelu_backward_kernel,
        grid=(length // rows,),
        in_specs=[
            pl.BlockSpec((rows, 2 * width), lambda i: (i, 0)),
            pl.BlockSpec((rows, width), lambda i: (i, 0)),
        ],
        out_specs=pl.BlockSpec((rows, 2 * width), lambda i: (i, 0)),
        out_shape=jax.ShapeDtypeStruct((length, 2 * width), bf16),
        compiler_params=pltpu.CompilerParams(vmem_limit_bytes=VMEM),
        cost_estimate=pl.CostEstimate(
            flops=length * width * 30, bytes_accessed=length * width * 16, transcendentals=length * width
        ),
        name="gelu_backward",
    )(gu, da)


def widen_kernel(in_ref, out_ref):
    out_ref[0] = in_ref[...].astype(f32)


def widen_parts(values, count, width):
    rows = values.shape[0]
    tile = min(rows, 512)
    return pl.pallas_call(
        widen_kernel,
        grid=(count, rows // tile),
        in_specs=[pl.BlockSpec((tile, width), lambda j, i: (i, j))],
        out_specs=pl.BlockSpec((1, tile, width), lambda j, i: (j, i, 0)),
        out_shape=jax.ShapeDtypeStruct((count, rows, width), f32),
        compiler_params=pltpu.CompilerParams(vmem_limit_bytes=VMEM),
        name="widen_parts",
    )(values)


def copy_kernel(order, in_ref, out_ref):
    out_ref[...] = in_ref[...]


def reorder(order, blocks):
    count, rows, cols = blocks.shape
    return pl.pallas_call(
        copy_kernel,
        grid_spec=pltpu.PrefetchScalarGridSpec(
            num_scalar_prefetch=1,
            grid=(count,),
            in_specs=[pl.BlockSpec((1, rows, cols), lambda i, order: (order[i], 0, 0))],
            out_specs=pl.BlockSpec((1, rows, cols), lambda i, order: (i, 0, 0)),
        ),
        out_shape=jax.ShapeDtypeStruct(blocks.shape, blocks.dtype),
        compiler_params=pltpu.CompilerParams(vmem_limit_bytes=VMEM),
        name="reorder",
    )(order, blocks)


MASKS = (0, 2, 4, 6, 1, 3, 5, 7)


class Ring:
    def __init__(self, n_seq, n_fsdp):
        self.n_seq, self.n_fsdp = n_seq, n_fsdp
        self.by_slot = n_seq == 8
        self.seq, self.fsdp = lax.axis_index("seq"), lax.axis_index("fsdp")
        places = jnp.arange(n_seq, dtype=jnp.int32)
        if self.by_slot:
            apart = places ^ self.seq
            self.order = (apart >> 1) + (apart & 1) * 4
            self.block_of_slot = jnp.array(MASKS, jnp.int32) ^ self.seq
        else:
            self.order = self.block_of_slot = places

    def swap(self, values, mask):
        return lax.ppermute(values, "seq", [(i, i ^ mask) for i in range(self.n_seq)])

    def turn(self, values, by):
        n = self.n_fsdp
        return lax.ppermute(values, "fsdp", [(i, (i + by) % n) for i in range(n)])

    def gather(self, values):
        if not self.by_slot:
            return lax.all_gather(values, "seq", axis=0, tiled=True)
        here = [values] + [self.swap(values, mask) for mask in MASKS[1:4]]
        return jnp.concatenate(here + [self.swap(block, 1) for block in here], axis=0)

    def scatter(self, away, near, length):
        if not self.by_slot:
            return [
                lax.psum_scatter(make(0, length), "seq", scatter_dimension=0, tiled=True)
                for make in near
            ]
        half, rows = length // 2, length // 8
        sent = [make(half, length).astype(bf16) for make in away]
        edges = [0]
        for part in sent:
            edges.append(edges[-1] + part.shape[1])
        spans = list(zip(edges[:-1], edges[1:]))
        arrived = self.swap(jnp.concatenate(sent, axis=1), 1)
        summed = [
            make(0, half) + arrived[:, low:high].astype(f32)
            for make, (low, high) in zip(near, spans)
        ]
        packed = jnp.concatenate([part.astype(bf16) for part in summed], axis=1)
        came = [self.swap(packed[k * rows : (k + 1) * rows], MASKS[k]) for k in (3, 1, 2)]
        return [
            sum([block[:, low:high].astype(f32) for block in came], part[:rows])
            for part, (low, high) in zip(summed, spans)
        ]

    def total_by_slot(self, values):
        if not self.by_slot:
            return lax.psum(values, "seq")
        slots = values.reshape(values.shape[0], 2, 2, 2, -1)
        for mask, dim in ((1, 1), (2, 3), (4, 2)):
            slots = slots + jnp.flip(self.swap(slots, mask), dim)
        return slots.reshape(values.shape)

    def total_seq(self, values):
        if not self.by_slot:
            return lax.psum(values, "seq")
        for mask in (1, 2, 4):
            values = values + self.swap(values, mask)
        return values

    def total_fsdp(self, values):
        return sum([self.turn(values, by) for by in range(1, self.n_fsdp)], values)

    def gather_fsdp(self, values):
        n = self.n_fsdp
        came = [values]
        for _ in range(n - 1):
            came.append(self.turn(came[-1], 1))
        doubled = jnp.stack((came[::-1] * 2)[:-1])
        return lax.dynamic_slice_in_dim(doubled, n - 1 - self.fsdp, n, 0)

    def scatter_fsdp(self, blocks):
        n = self.n_fsdp

        def block(back):
            place = lax.rem(self.fsdp + n - back, n)
            return lax.dynamic_index_in_dim(blocks, place, 0, False).astype(f32)

        total = block(1)
        for back in range(2, n + 1):
            total = block(back) + self.turn(total.astype(bf16), 1).astype(f32)
        return total

    def gather_all(self, values):
        rows, cols = values.shape
        along = self.gather_fsdp(values).reshape(1, -1, cols)
        if self.by_slot:
            full = reorder(self.order, self.gather(along))
        else:
            full = self.gather(along)
        return full.reshape(-1, rows, cols)


def pack(arrays, lead=0):
    parts, spans, start = [], [], 0
    for item in arrays:
        head = item.shape[:lead]
        flat = item.reshape(head + (-1,))
        rows = -(-flat.shape[-1] // 128)
        flat = jnp.pad(flat, [(0, 0)] * lead + [(0, rows * 128 - flat.shape[-1])])
        parts.append(flat.reshape(head + (rows, 128)))
        spans.append((start, rows, item.shape[lead:]))
        start += rows
    fill = -start % 16
    if fill:
        parts.append(jnp.zeros(parts[0].shape[:lead] + (fill, 128), parts[0].dtype))
    return jnp.concatenate(parts, axis=lead), spans


def unpack(packed, span):
    start, rows, shape = span
    lead = packed.shape[:-2]
    size = math.prod(shape)
    return packed[..., start : start + rows, :].reshape(lead + (-1,))[..., :size].reshape(lead + shape)


def rms_norm(values, gain):
    return values * lax.rsqrt(jnp.mean(values * values, axis=-1, keepdims=True) + epsilon) * gain


def matmul(left, right):
    return jnp.dot(left, right, preferred_element_type=f32)


def matmul_nt(left, right):
    return lax.dot_general(left, right, (((1,), (1,)), ((), ())), preferred_element_type=f32)


def matmul_tn(left, right):
    return lax.dot_general(left, right, (((0,), (0,)), ((), ())), preferred_element_type=f32)


def interleave(wide, narrow, count):
    a, b = wide.shape[1] // count, narrow.shape[1] // count
    return jnp.concatenate(
        [
            part
            for i in range(count)
            for part in (wide[:, i * a : (i + 1) * a], narrow[:, i * b : (i + 1) * b])
        ],
        axis=1,
    )


def separate(values, wide, count):
    a, step = wide // count, values.shape[1] // count
    first = [values[:, i * step : i * step + a] for i in range(count)]
    second = [values[:, i * step + a : (i + 1) * step] for i in range(count)]
    return jnp.concatenate(first, axis=1), jnp.concatenate(second, axis=1)


def side_by_side(stacked):
    return jnp.concatenate([stacked[i] for i in range(stacked.shape[0])], axis=1)


def run(
    n_seq,
    n_fsdp,
    hidden,
    embedded,
    segment,
    position,
    attn_gain,
    query_key_value_weight,
    query_key_value_down,
    query_key_value_up,
    out_weight,
    mlp_gain,
    gate_up_weight,
    feedforward_down_weight,
    feedforward_up_weight,
    down_weight,
    scan_gain,
    zx_weight,
    bc_weight,
    dt_weight,
    conv_x,
    conv_bc,
    dt_bias,
    decay_rate,
    skip_gain,
    inner_gain,
    out_proj,
    cotangent,
):
    ring = Ring(n_seq, n_fsdp)
    rows = hidden.shape[1]
    length = rows * n_seq
    attn_width = query_key_value_weight.shape[2]
    ff_width = gate_up_weight.shape[2]
    ff_rows = gate_up_weight.shape[1]
    scan_width = zx_weight.shape[2]
    scan_heads = dt_bias.shape[0]

    def scatter(*makes):
        return ring.scatter(makes, makes, length)

    def gather_weight(local, dim):
        return lax.all_gather(local, "fsdp", axis=dim, tiled=True)

    qkv_rows, out_rows, out_cols = query_key_value_weight.shape[1], *out_weight.shape
    out_cut = out_rows * out_cols // qkv_rows
    out_runs = out_cols // out_cut
    qkv_here = side_by_side(query_key_value_weight)
    out_here = jnp.concatenate(
        [out_weight[:, i * out_cut : (i + 1) * out_cut] for i in range(out_runs)]
    )
    qkv_here, out_here = lax.optimization_barrier((qkv_here, out_here))
    qkv_full = gather_weight(jnp.concatenate([qkv_here, out_here], axis=1), 0)
    out_full = qkv_full[:, 3 * attn_width :].reshape(n_fsdp, out_runs, out_rows, out_cut)
    out_full = out_full.transpose(2, 0, 1, 3).reshape(out_rows, -1)
    qkv_full = qkv_full[:, : 3 * attn_width]
    gate_full = gather_weight(
        jnp.concatenate(
            [side_by_side(gate_up_weight), side_by_side(feedforward_up_weight)], axis=0
        ),
        0,
    )
    down_full = gather_weight(down_weight, 1)
    zx_full = gather_weight(side_by_side(zx_weight), 0)
    proj_full = gather_weight(out_proj, 1)

    packed, spans = pack(
        [
            query_key_value_down,
            feedforward_down_weight,
            bc_weight,
            attn_gain,
            mlp_gain,
            scan_gain,
            conv_bc,
        ]
    )
    everywhere = ring.gather_all(packed)
    shared = [unpack(everywhere, span) for span in spans]
    attention_down = shared[0].reshape(-1, 3 * ADAPTER_RANK)
    feedforward_down = shared[1].reshape(-1, ADAPTER_RANK)
    bc_full = shared[2].reshape(-1, 256)
    gain_one, gain_two, gain_three = (item.reshape(-1).astype(f32) for item in shared[3:6])
    taps_bc = shared[6].transpose(1, 0, 2).reshape(4, -1).astype(f32)
    packed, spans = pack(
        [query_key_value_up, dt_weight, conv_x, inner_gain]
    )
    along = ring.gather_fsdp(packed)
    shared = [unpack(along, span) for span in spans]
    qkv_up = shared[0].transpose(1, 0, 2, 3).reshape(3, ADAPTER_RANK, attn_width)
    dt_full = jnp.pad(shared[1].reshape(-1, scan_heads), ((0, 0), (0, 128 - scan_heads)))
    taps_x = shared[2].transpose(1, 0, 2).reshape(4, scan_width).astype(f32)
    inner_scale = shared[3].reshape(1, scan_width).astype(f32)
    lift = jnp.concatenate(
        [
            jnp.pad(
                qkv_up[part], ((0, 0), (part * attn_width, (2 - part) * attn_width))
            )
            for part in range(3)
        ],
        axis=0,
    )
    head_terms = jnp.pad(
        jnp.stack([dt_bias, decay_rate, skip_gain]), ((0, 5), (0, 128 - scan_heads))
    )

    marks_all = ring.gather(jnp.stack([segment[0], position[0]])[None])
    seg_slots, pos_slots = marks_all[:, 0], marks_all[:, 1]
    natural = (ring.order[:, None] == jnp.arange(n_seq)[None, :])[:, :, None]
    seg_natural = jnp.sum(jnp.where(natural, seg_slots[None], 0), axis=1).reshape(-1)
    scan_mark, scan_seg = scan_marks(seg_natural)
    places = ring.block_of_slot[:, None] * rows + jnp.arange(rows, dtype=jnp.int32)[None]
    row_info = jnp.stack([places.reshape(-1), seg_slots.reshape(-1)], axis=1).astype(f32)
    col_info = jnp.pad(row_info.T, ((0, 6), (0, 0)))
    cosine, sine = rope_tables(pos_slots.reshape(-1))

    hidden_rows = hidden[0].astype(f32)
    joined = jnp.concatenate([hidden_rows, embedded[0].astype(f32)], axis=1)
    normed, norm_pull_one = jax.vjp(rms_norm, joined, gain_one)
    normed_low = normed.astype(bf16)
    attn_rows = ring.gather(normed_low)
    lora_rows = matmul(attn_rows, attention_down).astype(bf16)
    cot_low = cotangent[0]
    cot_rows = ring.gather(cot_low)
    (
        lora_rows,
        cot_rows,
        lift,
        dt_full,
        taps_x,
        taps_bc,
        inner_scale,
        head_terms,
        scan_mark,
        scan_seg,
        row_info,
        col_info,
        cosine,
        sine,
        bc_full,
        feedforward_down,
    ) = lax.optimization_barrier(
        (
            lora_rows,
            cot_rows,
            lift,
            dt_full,
            taps_x,
            taps_bc,
            inner_scale,
            head_terms,
            scan_mark,
            scan_seg,
            row_info,
            col_info,
            cosine,
            sine,
            bc_full,
            feedforward_down,
        )
    )
    projected = matmul(attn_rows, qkv_full) + matmul(lora_rows, lift)
    query, key, value, mixed, lse = attention_forward(projected, cosine, sine, row_info, col_info)
    mixed_low = mixed.astype(bf16)
    first = hidden_rows + scatter(lambda a, b: matmul(mixed_low[a:b], out_full))[0]

    mlp_in, norm_pull_two = jax.vjp(rms_norm, first, gain_two)
    mlp_low = mlp_in.astype(bf16)
    mlp_lora_low = matmul(mlp_low, feedforward_down).astype(bf16)
    mlp_rows = ring.gather(interleave(mlp_low, mlp_lora_low, n_fsdp))
    gate_and_up = matmul(mlp_rows, gate_full)
    activated = jax.nn.gelu(gate_and_up[:, :ff_width]) * gate_and_up[:, ff_width:]
    activated_low = activated.astype(bf16)
    second = first + scatter(lambda a, b: matmul(activated_low[a:b], down_full))[0]

    scan_in, norm_pull_three = jax.vjp(rms_norm, second, gain_three)
    scan_low = scan_in.astype(bf16)
    scan_rows = ring.gather(scan_low)
    side_full = jnp.concatenate([dt_full, bc_full], axis=1)
    bc_rows = matmul(scan_rows, bc_full).astype(bf16).astype(f32)
    zx = matmul(scan_rows, zx_full)
    step_raw = matmul(scan_rows, dt_full)
    mixer, states = scan_forward(
        ring.order, zx, step_raw, bc_rows, scan_mark, scan_seg, taps_x, taps_bc, head_terms
    )
    gated = mixer * jax.nn.silu(zx[:, :scan_width])
    squares = ring.total_by_slot(jnp.sum(gated * gated, axis=1)[None])[0]
    inv_rms = lax.rsqrt(squares / DI + epsilon)
    scan_norm_low = (gated * inv_rms[:, None] * inner_scale).astype(bf16)
    proj_grad = matmul_tn(scan_norm_low, cot_rows).astype(bf16)
    proj_grad, proj_full = lax.optimization_barrier((proj_grad, proj_full))
    grad_norm = matmul_nt(cot_rows, proj_full)
    cross = ring.total_by_slot(jnp.sum(grad_norm * inner_scale * gated, axis=1)[None])[0]
    row_terms = jnp.pad(jnp.stack([inv_rms, inv_rms**3 / DI * cross]), ((0, 6), (0, 0)))
    grad_third = cot_low.astype(f32)
    g_out_proj = lax.psum_scatter(proj_grad, "fsdp", scatter_dimension=1, tiled=True)
    grad_zx, grad_side, conv_x_grad, conv_bc_grad, head_grad, inner_grad = scan_backward(
        ring.order,
        zx,
        step_raw,
        bc_rows,
        scan_mark,
        scan_seg,
        taps_x,
        taps_bc,
        head_terms,
        mixer,
        states,
        grad_norm,
        row_terms,
        inner_scale,
    )
    zx_grad = matmul_tn(scan_rows, grad_zx).astype(bf16)
    g_zx = lax.psum_scatter(zx_grad, "fsdp", scatter_dimension=0, tiled=True)
    zx_grad, grad_zx_near = lax.optimization_barrier((zx_grad, grad_zx))

    def back_of(grad):
        return lambda a, b: matmul_nt(grad[a:b], zx_full) + matmul_nt(grad_side[a:b], side_full)

    (back_three,) = ring.scatter((back_of(grad_zx),), (back_of(grad_zx_near),), length)
    back_three, g_out_proj = lax.optimization_barrier((back_three, g_out_proj))
    second_part, gain_three_grad = norm_pull_three(back_three)
    grad_second = grad_third + second_part

    second_rows = ring.gather(grad_second.astype(bf16))
    down_grad = matmul_tn(activated_low, second_rows).astype(bf16)
    down_grad, second_rows, g_zx = lax.optimization_barrier((down_grad, second_rows, g_zx))
    grad_activated = matmul_nt(second_rows, down_full)
    g_down = lax.psum_scatter(down_grad, "fsdp", scatter_dimension=1, tiled=True)
    grad_gate = gelu_backward(gate_and_up, grad_activated)
    gate_grad = matmul_tn(mlp_rows, grad_gate).astype(bf16)
    gate_grad, grad_gate_near = lax.optimization_barrier((gate_grad, grad_gate))
    g_gate = lax.psum_scatter(gate_grad, "fsdp", scatter_dimension=0, tiled=True)
    back_two = ring.scatter(
        (lambda a, b: matmul_nt(grad_gate[a:b], gate_full),),
        (lambda a, b: matmul_nt(grad_gate_near[a:b], gate_full),),
        length,
    )
    back_two, back_two_lora = separate(back_two[0], MODEL_WIDTH, n_fsdp)
    mlp_lora_grad = back_two_lora.astype(bf16)
    first_part, gain_two_grad = norm_pull_two(
        back_two + matmul_nt(mlp_lora_grad, feedforward_down)
    )
    grad_first = grad_second + first_part

    first_low, g_down = lax.optimization_barrier((grad_first.astype(bf16), g_down))
    first_rows = ring.gather(first_low)
    grad_mixed = matmul_nt(first_rows, out_full).astype(bf16)
    out_grad = matmul_tn(mixed_low, first_rows).astype(bf16)
    out_grad = out_grad.reshape(out_rows, n_fsdp, out_runs, out_cut).transpose(1, 2, 0, 3)
    out_grad = out_grad.reshape(-1, out_cut)
    grad_projected = attention_backward(
        query, key, value, grad_mixed, mixed, lse, cosine, sine, row_info, col_info
    )
    qkv_grad = matmul_tn(attn_rows, grad_projected).astype(bf16)
    qkv_grad = jnp.concatenate([qkv_grad, out_grad], axis=1)
    qkv_grad, g_gate = lax.optimization_barrier((qkv_grad, g_gate))
    g_qkv = lax.psum_scatter(qkv_grad, "fsdp", scatter_dimension=0, tiled=True)
    g_out = g_qkv[:, 3 * attn_width :].reshape(out_runs, out_rows, out_cut)
    g_out = jnp.concatenate([g_out[i] for i in range(out_runs)], axis=1)
    lift_grad = matmul_tn(lora_rows, grad_projected)
    lift_grad = jnp.stack(
        [
            lift_grad[
                part * ADAPTER_RANK : (part + 1) * ADAPTER_RANK,
                part * attn_width : (part + 1) * attn_width,
            ]
            for part in range(3)
        ]
    )
    back_one, lora_grad = scatter(
        lambda a, b: matmul_nt(grad_projected[a:b], qkv_full),
        lambda a, b: matmul_nt(grad_projected[a:b], lift),
    )
    lora_grad_low = lora_grad.astype(bf16)
    grad_joined, gain_one_grad = norm_pull_one(
        back_one + matmul_nt(lora_grad_low, attention_down)
    )
    grad_hidden = (grad_first + grad_joined[:, :MODEL_WIDTH])[None]
    grad_embedded = grad_joined[:, MODEL_WIDTH:][None]
    grad_side, lora_grad_low = lax.optimization_barrier((grad_side, lora_grad_low))
    dt_grad = matmul_tn(scan_rows, grad_side[:, :128])[:, :scan_heads]
    grad_bc_low = scatter(lambda a, b: grad_side[a:b, 128:].astype(f32))[0].astype(bf16)
    small_rows = ring.gather(
        jnp.concatenate([lora_grad_low, mlp_lora_grad, grad_bc_low], axis=1)
    )
    lora_grad_rows = small_rows[:, : 3 * ADAPTER_RANK]
    mlp_lora_grad_rows = small_rows[:, 3 * ADAPTER_RANK : 4 * ADAPTER_RANK]
    grad_bc_rows = small_rows[:, 4 * ADAPTER_RANK :]

    scan_norm_late, _ = lax.optimization_barrier((scan_norm_low, lora_grad_low))
    third = second + scatter(lambda a, b: matmul(scan_norm_late[a:b], proj_full))[0]
    output = third.astype(bf16)[None]

    def share(values_rows, grad_rows):
        wide = values_rows.shape[1] // n_seq
        cut = lax.dynamic_slice_in_dim(values_rows, ring.seq * wide, wide, 1)
        return matmul_tn(cut, grad_rows).astype(bf16).reshape(n_fsdp, wide // n_fsdp, -1)

    def share_interleaved(values_rows, grad_rows):
        wide = MODEL_WIDTH // n_seq
        runs = values_rows.reshape(length, n_fsdp, -1)[:, :, : MODEL_WIDTH // n_fsdp]
        run = lax.dynamic_index_in_dim(runs, ring.seq * n_fsdp // n_seq, 1, False)
        at = lax.rem(ring.seq, n_seq // n_fsdp) * wide
        cut = lax.dynamic_slice_in_dim(run, at, wide, 1)
        return matmul_tn(cut, grad_rows).astype(bf16).reshape(n_fsdp, wide // n_fsdp, -1)

    def by_fsdp(grad, dim):
        shape = grad.shape[:dim] + (n_fsdp, grad.shape[dim] // n_fsdp) + grad.shape[dim + 1 :]
        return jnp.moveaxis(grad.astype(bf16).reshape(shape), dim, 0)

    packed, spans = pack(
        [
            share(scan_rows, grad_bc_rows),
            by_fsdp(dt_grad, 0),
            by_fsdp(conv_x_grad[:4], 1),
            by_fsdp(inner_grad[0], 0),
            share(attn_rows, lora_grad_rows),
            by_fsdp(lift_grad, 1),
            share_interleaved(mlp_rows, mlp_lora_grad_rows),
        ],
        1,
    )
    mine = ring.scatter_fsdp(packed)
    g_bc, g_dt, g_conv_x, g_inner, g_qkv_down, g_qkv_up, g_mlp_down = (
        unpack(mine, span) for span in spans
    )
    g_heads = ring.total_fsdp(head_grad)
    g_bias, g_rate, g_skip = (g_heads[i, :scan_heads] for i in range(3))
    gains = jnp.concatenate(
        [gain_one_grad, gain_two_grad, gain_three_grad, conv_bc_grad[:4].reshape(-1)]
    )
    gains = ring.total_fsdp(ring.total_seq(gains.reshape(-1, 128))).reshape(-1)
    own = ring.seq * n_fsdp + ring.fsdp
    count = n_seq * n_fsdp

    def own_part(values):
        size = values.shape[-1] // count
        return lax.dynamic_slice_in_dim(values, own * size, size, values.ndim - 1)

    joined_width = 2 * MODEL_WIDTH
    g_attn_gain = own_part(gains[:joined_width])
    g_mlp_gain = own_part(gains[joined_width : joined_width + MODEL_WIDTH])
    g_scan_gain = own_part(gains[joined_width + MODEL_WIDTH : joined_width + 2 * MODEL_WIDTH])
    g_conv_bc = own_part(gains[joined_width + 2 * MODEL_WIDTH :].reshape(4, -1))

    def apart(grad, count):
        wide = grad.shape[1] // count
        return jnp.stack([grad[:, i * wide : (i + 1) * wide] for i in range(count)]).astype(f32)

    return (
        output,
        grad_hidden,
        grad_embedded,
        g_attn_gain,
        widen_parts(g_qkv, 3, attn_width),
        g_qkv_down,
        g_qkv_up,
        g_out.astype(f32),
        g_mlp_gain,
        apart(g_gate[:ff_rows], 2),
        g_mlp_down,
        apart(g_gate[ff_rows:], 2),
        g_down.astype(f32),
        g_scan_gain,
        apart(g_zx, 2),
        g_bc,
        g_dt,
        g_conv_x,
        g_conv_bc,
        g_bias,
        g_rate,
        g_skip,
        g_inner,
        g_out_proj.astype(f32),
    )


def solution(mesh):
    return jax.shard_map(
        functools.partial(run, mesh.shape["seq"], mesh.shape["fsdp"]),
        mesh=mesh,
        in_specs=(
            P("fsdp", "seq", None),
            P("fsdp", "seq", None),
            P("fsdp", "seq"),
            P("fsdp", "seq"),
            P(("seq", "fsdp")),
            P(None, "fsdp", "seq"),
            P(("seq", "fsdp"), None),
            P(None, "fsdp", "seq"),
            P("seq", "fsdp"),
            P(("seq", "fsdp")),
            P(None, "fsdp", "seq"),
            P(("seq", "fsdp"), None),
            P(None, "fsdp", "seq"),
            P("seq", "fsdp"),
            P(("seq", "fsdp")),
            P(None, "fsdp", "seq"),
            P(("seq", "fsdp"), None),
            P("fsdp", "seq"),
            P(None, ("seq", "fsdp")),
            P(None, ("seq", "fsdp")),
            P("seq"),
            P("seq"),
            P("seq"),
            P(("seq", "fsdp")),
            P("seq", "fsdp"),
            P("fsdp", "seq", None),
        ),
        out_specs=(
            P("fsdp", "seq", None),
            P("fsdp", "seq", None),
            P("fsdp", "seq", None),
            P(("seq", "fsdp")),
            P(None, "fsdp", "seq"),
            P(("seq", "fsdp"), None),
            P(None, "fsdp", "seq"),
            P("seq", "fsdp"),
            P(("seq", "fsdp")),
            P(None, "fsdp", "seq"),
            P(("seq", "fsdp"), None),
            P(None, "fsdp", "seq"),
            P("seq", "fsdp"),
            P(("seq", "fsdp")),
            P(None, "fsdp", "seq"),
            P(("seq", "fsdp"), None),
            P("fsdp", "seq"),
            P(None, ("seq", "fsdp")),
            P(None, ("seq", "fsdp")),
            P("seq"),
            P("seq"),
            P("seq"),
            P(("seq", "fsdp")),
            P("seq", "fsdp"),
        ),
        check_vma=False,
    )
```

```python
import functools
import math

import jax
import jax.numpy as jnp
from jax import lax
from jax.experimental import pallas as pl
from jax.experimental.pallas import tpu as pltpu
from jax.sharding import PartitionSpec as P

MODEL_WIDTH = 2048
ADAPTER_RANK = 128
DI = 4096
epsilon = 1e-06

f32 = jnp.float32
bf16 = jnp.bfloat16
T = 128
HS = 64
VMEM = 48 * 1024 * 1024


def dot(a, b, ca, cb):
    return lax.dot_general(
        a.astype(bf16), b.astype(bf16), (((ca,), (cb,)), ((), ())), preferred_element_type=f32
    )


def masked_sum(mask, values):
    high = values.astype(bf16)
    rest = values - high.astype(f32)
    middle = rest.astype(bf16)
    low = (rest - middle.astype(f32)).astype(bf16)
    wide = mask.astype(bf16)
    return dot(
        jnp.concatenate([wide, wide, wide], axis=1),
        jnp.concatenate([high, middle, low], axis=0),
        1,
        0,
    )


def sigmoid(v):
    return 1.0 / (1.0 + jnp.exp(-v))


def iota(shape, dim):
    return lax.broadcasted_iota(jnp.int32, shape, dim)


def spread_heads(per_head, width):
    rows = per_head.shape[0]
    low = iota((rows, 2 * HS), 1) < HS
    return jnp.concatenate(
        [
            jnp.where(low, per_head[:, 2 * j : 2 * j + 1], per_head[:, 2 * j + 1 : 2 * j + 2])
            for j in range(width // (2 * HS))
        ],
        axis=1,
    )


def sum_heads_once(values):
    width = values.shape[1]
    return dot(values, iota((width, 128), 0) // HS == iota((width, 128), 1), 1, 0)


def sum_heads(values):
    width = values.shape[1]
    member = (iota((width, 128), 0) // HS == iota((width, 128), 1)).astype(bf16)
    high = values.astype(bf16)
    low = (values - high.astype(f32)).astype(bf16)
    return dot(high, member, 1, 0) + dot(low, member, 1, 0)


def shift_down(values, tail, by):
    moved = pltpu.roll(values, by, 0)
    first = jnp.where(iota(tail.shape, 0) < by, pltpu.roll(tail, by, 0), moved[:8])
    return jnp.concatenate([first, moved[8:]], axis=0)


def shift_up(values, head, by):
    size = values.shape[0]
    moved = pltpu.roll(values, size - by, 0)
    last = jnp.where(iota(head.shape, 0) >= 8 - by, pltpu.roll(head, 8 - by, 0), moved[size - 8 :])
    return jnp.concatenate([moved[: size - 8], last], axis=0)


def conv(values, tail, taps, marks):
    result = values * taps[0:1]
    for k in range(1, 4):
        result = result + shift_down(values, tail, k) * marks[:, k - 1 : k] * taps[k : k + 1]
    return result


def block_terms(steps_raw, marks, seg_row, bias, rate):
    steps = steps_raw + bias
    steps = jnp.maximum(steps, 0.0) + jnp.log1p(jnp.exp(-jnp.abs(steps)))
    lower = iota((T, T), 1) <= iota((T, T), 0)
    running = masked_sum(lower, -steps * rate)
    allowed = lower & (marks[:, 6:7] == seg_row)
    entering = jnp.exp(running) * marks[:, 3:4]
    ending = jnp.exp(running[T - 1 : T] - running) * marks[:, 4:5]
    kept = jnp.exp(running[T - 1 : T]) * marks[T - 1 : T, 5:6]
    return steps, running, allowed, entering, ending, kept


def decay_of(running, running_t, allowed, m):
    spread = running[:, m : m + 1] - running_t[m : m + 1, :]
    return jnp.where(allowed, jnp.exp(jnp.minimum(spread, 0.0)), 0.0)


def scan_forward_kernel(
    order, x_ref, step_ref, bc_ref, mark_ref, seg_ref, tapx_ref, tapbc_ref, head_ref,
    y_ref, states_ref, state, tail_x, tail_bc,
):
    block = pl.program_id(0)

    @pl.when(block == 0)
    def _():
        state[...] = jnp.zeros_like(state)
        tail_x[...] = jnp.zeros_like(tail_x)
        tail_bc[...] = jnp.zeros_like(tail_bc)

    width = x_ref.shape[1]
    marks = mark_ref[...]
    x = x_ref[...]
    xs = conv(x, tail_x[...], tapx_ref[...], marks)
    xs = xs * sigmoid(xs)
    tail_x[...] = x[T - 8 :]
    bc = bc_ref[...]
    bcs = conv(bc, tail_bc[...], tapbc_ref[...], marks)
    bcs = bcs * sigmoid(bcs)
    tail_bc[...] = bc[T - 8 :]
    b_rows, c_rows = bcs[:, :128], bcs[:, 128:]
    bias, rate, skip = head_ref[0:1], head_ref[1:2], head_ref[2:3]
    steps, running, allowed, entering, ending, kept = block_terms(
        step_ref[...], marks, seg_ref[0], bias, rate
    )
    running_t, steps_t = running.T, steps.T
    inner = dot(c_rows, b_rows, 1, 1)
    held = state[...]
    states_ref[0] = held
    carried = dot(c_rows, held, 1, 0)
    low = iota((T, 2 * HS), 1) < HS
    parts = []
    for j in range(width // (2 * HS)):
        pair = xs[:, 2 * HS * j : 2 * HS * (j + 1)].astype(bf16)
        made = [
            dot(decay_of(running, running_t, allowed, m) * inner * steps_t[m : m + 1], pair, 1, 0)
            for m in (2 * j, 2 * j + 1)
        ]
        parts.append(jnp.where(low, made[0], made[1]))
    local = jnp.concatenate(parts, axis=1)
    y_ref[...] = local + carried * spread_heads(entering, width) + xs * spread_heads(skip, width)
    leaving = spread_heads(ending * steps, width) * xs
    state[...] = held * spread_heads(kept, width) + dot(b_rows, leaving, 0, 0)


def scan_backward_kernel(
    order, x_ref, xt_ref, z_ref, step_ref, bc_ref, bct_ref, mark_ref, seg_ref, tapx_ref, tapbc_ref,
    head_ref, y_ref, states_ref, gn_ref, row_ref, inner_ref,
    gzx_ref, gside_ref, gtapx_ref, gtapbc_ref, ghead_ref, ginner_ref,
    d_state, cols, next_x, next_bc,
):
    @pl.when(pl.program_id(0) == 0)
    def _():
        for ref in (d_state, cols, next_x, next_bc, gtapx_ref, gtapbc_ref, ghead_ref, ginner_ref):
            ref[...] = jnp.zeros_like(ref)

    width = x_ref.shape[1]
    marks = mark_ref[...]
    tapx, tapbc = tapx_ref[...], tapbc_ref[...]
    x, tail_x = x_ref[...], xt_ref[...]
    xc = conv(x, tail_x, tapx, marks)
    xsig = sigmoid(xc)
    xs = xc * xsig
    bc, tail_bc = bc_ref[...], bct_ref[...]
    bcc = conv(bc, tail_bc, tapbc, marks)
    bcsig = sigmoid(bcc)
    bcs = bcc * bcsig
    b_rows, c_rows = bcs[:, :128].astype(bf16), bcs[:, 128:].astype(bf16)
    bias, rate, skip = head_ref[0:1], head_ref[1:2], head_ref[2:3]
    steps, running, allowed, entering, ending, kept = block_terms(
        step_ref[...], marks, seg_ref[0], bias, rate
    )
    running_t, steps_t = running.T, steps.T

    z, y, gn = z_ref[...], y_ref[...], gn_ref[...]
    row_terms = row_ref[...].T
    inv, cross = row_terms[:, 0:1], row_terms[:, 1:2]
    zsig = sigmoid(z)
    zs = z * zsig
    gated = y * zs
    ginner_ref[...] += jnp.sum(gn * gated * inv, axis=0, keepdims=True)
    g_gated = gn * inner_ref[...] * inv - gated * cross
    gzx_ref[:, :width] = (g_gated * y * (zsig + zs * (1.0 - zsig))).astype(bf16)
    dy = g_gated * zs

    inner = dot(c_rows, b_rows, 1, 1)
    held = states_ref[0]
    held_low = held.astype(bf16)
    ds = d_state[...]
    ds_low = ds.astype(bf16)
    entering_wide = spread_heads(entering, width)
    leaving_wide = spread_heads(ending * steps, width)
    kept_wide = spread_heads(kept, width)

    low = iota((T, 2 * HS), 1) < HS
    lane = iota((T, 128), 1)
    d_inner = jnp.zeros((T, T), f32)
    rows = jnp.zeros((T, 128), f32)
    parts = []
    for j in range(width // (2 * HS)):
        cut = slice(2 * HS * j, 2 * HS * (j + 1))
        x_pair = xs[:, cut].astype(bf16)
        dy_pair = dy[:, cut]
        dy_low = dy_pair.astype(bf16)
        made = []
        for m in (2 * j, 2 * j + 1):
            mine = low if m % 2 == 0 else ~low
            decay = decay_of(running, running_t, allowed, m)
            grown = decay * steps_t[m : m + 1]
            d_weight = dot(jnp.where(mine, dy_pair, 0.0), x_pair, 1, 1)
            d_inner = d_inner + d_weight * grown
            pushed = d_weight * decay * inner
            cols[m : m + 1, :] = jnp.sum(pushed, axis=0, keepdims=True)
            rows = rows + jnp.where(
                lane == m, jnp.sum(pushed * steps_t[m : m + 1], axis=1, keepdims=True), 0.0
            )
            made.append(dot(grown * inner, dy_low, 0, 0))
        parts.append(jnp.where(low, made[0], made[1]))
    v_rows = dot(b_rows, ds_low, 1, 0)
    dxs = jnp.concatenate(parts, axis=1) + dy * spread_heads(skip, width) + leaving_wide * v_rows
    u_rows = (dy * entering_wide).astype(bf16)
    carried = dot(c_rows, held_low, 1, 0)
    d_c = dot(d_inner, b_rows, 1, 0) + dot(u_rows, held_low, 1, 1)
    d_b = dot(d_inner, c_rows, 0, 0) + dot(leaving_wide * xs, ds_low, 1, 1)
    d_step = cols[...].T
    d_running = rows - d_step * steps
    d_running = d_running + sum_heads_once(dy * carried) * entering
    d_ending = sum_heads_once(v_rows * xs)
    d_step = d_step + d_ending * ending
    moved = d_ending * ending * steps
    d_kept = sum_heads(jnp.broadcast_to(jnp.sum(ds * held, axis=0, keepdims=True), (8, width)))
    last = jnp.sum(moved, axis=0, keepdims=True) + d_kept[0:1] * kept
    d_running = d_running - moved + jnp.where(iota((T, 128), 0) == T - 1, last, 0.0)
    d_log = masked_sum(iota((T, T), 1) >= iota((T, T), 0), d_running)
    d_step = d_step - rate * d_log
    d_raw = d_step * sigmoid(step_ref[...] + bias)
    gside_ref[:, :128] = d_raw.astype(bf16)
    d_skip = sum_heads(
        jnp.broadcast_to(jnp.sum(dy * xs, axis=0, keepdims=True), (8, width))
    )
    ghead_ref[0:1] += jnp.sum(d_raw, axis=0, keepdims=True)
    ghead_ref[1:2] -= jnp.sum(steps * d_log, axis=0, keepdims=True)
    ghead_ref[2:3] += d_skip[0:1]
    d_state[...] = ds * kept_wide + dot(c_rows, u_rows, 0, 0)

    def conv_back(grad, values, tail, taps, following, gtap_ref):
        result = grad * taps[0:1]
        gtap_ref[0:1] += jnp.sum(grad * values, axis=0, keepdims=True)
        for k in range(1, 4):
            marked = grad * marks[:, k - 1 : k]
            gtap_ref[k : k + 1] += jnp.sum(
                marked * shift_down(values, tail, k), axis=0, keepdims=True
            )
            sent = marked * taps[k : k + 1]
            result = result + shift_up(sent, following[k - 1], k)
            following[k - 1] = sent[:8]
        return result

    dxc = dxs * (xsig + xs * (1.0 - xsig))
    gzx_ref[:, width:] = conv_back(dxc, x, tail_x, tapx, next_x, gtapx_ref).astype(bf16)
    dbc = jnp.concatenate([d_b, d_c], axis=1) * (bcsig + bcs * (1.0 - bcsig))
    gside_ref[:, 128:] = conv_back(dbc, bc, tail_bc, tapbc, next_bc, gtapbc_ref).astype(bf16)


def scan_marks(seg):
    length = seg.shape[0]
    blocks = seg.reshape(-1, T)
    last = jnp.concatenate([jnp.full((1,), -1, seg.dtype), blocks[:-1, -1]])
    cols = []
    for k in range(1, 4):
        earlier = jnp.pad(seg, (k, 0), constant_values=-1)[:-k]
        cols.append(earlier == seg)
    cols.append((blocks == last[:, None]).reshape(length))
    cols.append((blocks == blocks[:, -1:]).reshape(length))
    cols.append(jnp.repeat(blocks[:, -1] == last, T))
    cols.append(seg)
    cols.append(seg)
    marks = jnp.stack([c.astype(f32) for c in cols], axis=1)
    return marks, blocks.astype(f32)[:, None, :]


def whole(shape):
    return pl.BlockSpec(shape, lambda *_: (0,) * len(shape))


def scan_forward(order, zx, step, bc, marks, seg_rows, tapx, tapbc, heads):
    length, width = zx.shape[0], zx.shape[1] // 2
    count = length // T

    def rows(cols, at=0):
        return pl.BlockSpec((T, cols), lambda i, order: (order[i], at))

    return pl.pallas_call(
        scan_forward_kernel,
        grid_spec=pltpu.PrefetchScalarGridSpec(
            num_scalar_prefetch=1,
            grid=(count,),
            in_specs=[
                rows(width, 1), rows(128), rows(256),
                pl.BlockSpec((T, 8), lambda i, order: (i, 0)),
                pl.BlockSpec((1, 1, T), lambda i, order: (i, 0, 0)),
                whole(tapx.shape), whole(tapbc.shape), whole(heads.shape),
            ],
            out_specs=[rows(width), pl.BlockSpec((1, 128, width), lambda i, order: (i, 0, 0))],
            scratch_shapes=[
                pltpu.VMEM((128, width), f32), pltpu.VMEM((8, width), f32), pltpu.VMEM((8, 256), f32),
            ],
        ),
        out_shape=[
            jax.ShapeDtypeStruct((length, width), f32),
            jax.ShapeDtypeStruct((count, 128, width), f32),
        ],
        compiler_params=pltpu.CompilerParams(vmem_limit_bytes=VMEM),
        cost_estimate=pl.CostEstimate(
            flops=length * width * 128 * 8, bytes_accessed=length * width * 16, transcendentals=length * width * 3
        ),
        name="scan_forward",
    )(order, zx, step, bc, marks, seg_rows, tapx, tapbc, heads)


def scan_backward(
    order, zx, step, bc, marks, seg_rows, tapx, tapbc, heads, y, states, gn, row_terms, inner
):
    length, width = zx.shape[0], zx.shape[1] // 2
    count = length // T

    def rows(cols, at=0):
        return pl.BlockSpec((T, cols), lambda i, order: (order[count - 1 - i], at))

    def tails(cols, at=0):
        return pl.BlockSpec(
            (8, cols),
            lambda i, order: (order[jnp.maximum(count - 2 - i, 0)] * (T // 8) + (T // 8 - 1), at),
        )

    return pl.pallas_call(
        scan_backward_kernel,
        grid_spec=pltpu.PrefetchScalarGridSpec(
            num_scalar_prefetch=1,
            grid=(count,),
            in_specs=[
                rows(width, 1), tails(width, 1), rows(width), rows(128), rows(256), tails(256),
                pl.BlockSpec((T, 8), lambda i, order: (count - 1 - i, 0)),
                pl.BlockSpec((1, 1, T), lambda i, order: (count - 1 - i, 0, 0)),
                whole(tapx.shape), whole(tapbc.shape), whole(heads.shape),
                rows(width),
                pl.BlockSpec((1, 128, width), lambda i, order: (count - 1 - i, 0, 0)),
                rows(width),
                pl.BlockSpec((8, T), lambda i, order: (0, order[count - 1 - i])),
                whole(inner.shape),
            ],
            out_specs=[
                rows(2 * width), rows(384),
                whole((8, width)), whole((8, 256)), whole((8, 128)), whole((1, width)),
            ],
            scratch_shapes=[
                pltpu.VMEM((128, width), f32), pltpu.VMEM((128, T), f32),
                pltpu.VMEM((3, 8, width), f32), pltpu.VMEM((3, 8, 256), f32),
            ],
        ),
        out_shape=[
            jax.ShapeDtypeStruct((length, 2 * width), bf16),
            jax.ShapeDtypeStruct((length, 384), bf16),
            jax.ShapeDtypeStruct((8, width), f32),
            jax.ShapeDtypeStruct((8, 256), f32),
            jax.ShapeDtypeStruct((8, 128), f32),
            jax.ShapeDtypeStruct((1, width), f32),
        ],
        compiler_params=pltpu.CompilerParams(vmem_limit_bytes=VMEM),
        cost_estimate=pl.CostEstimate(
            flops=length * width * 128 * 20, bytes_accessed=length * width * 32, transcendentals=length * width * 3
        ),
        name="scan_backward",
    )(order, zx, zx, zx, step, bc, bc, marks, seg_rows, tapx, tapbc, heads, y, states, gn, row_terms, inner)


BQ = 256


def attention_forward_kernel(
    q_ref, k_ref, v_ref, cos_ref, sin_ref, row_ref, col_ref,
    qr_ref, kr_ref, vr_ref, mixed_ref, lse_ref, bias,
):
    i, h = pl.program_id(0), pl.program_id(1)
    rows = q_ref.shape[0]
    lanes = pl.ds(pl.multiple_of(h * 128, 128), 128)

    def turn(values, cosine, sine):
        return values * cosine + pltpu.roll(values, 64, 1) * sine

    @pl.when(h == 0)
    def _():
        allowed = (col_ref[0:1] <= row_ref[:, 0:1]) & (col_ref[1:2] == row_ref[:, 1:2])
        bias[...] = jnp.where(allowed, 0.0, -1e30)

    @pl.when(i == 0)
    def _():
        kr_ref[:, lanes] = turn(k_ref[...], cos_ref[...], sin_ref[...]).astype(bf16)
        vr_ref[:, lanes] = v_ref[...].astype(bf16)

    here = pl.ds(pl.multiple_of(i * rows, rows), rows)
    q = turn(q_ref[...], cos_ref[here, :], sin_ref[here, :]).astype(bf16)
    qr_ref[...] = q
    scores = dot(q, kr_ref[:, lanes], 1, 1) * (128 ** -0.5) + bias[...]
    largest = jnp.max(scores, axis=1, keepdims=True)
    terms = jnp.exp(scores - largest)
    total = jnp.sum(terms, axis=1, keepdims=True)
    probs = (terms * (1.0 / total)).astype(bf16)
    mixed_ref[...] = dot(probs, vr_ref[:, lanes], 1, 0)
    lse = largest + jnp.log(total)
    lse_ref[...] = jnp.where(iota((rows, 128), 1) == h, lse, lse_ref[...])


def attention_backward_kernel(
    q_ref, k_ref, v_ref, do_ref, mixed_ref, lse_ref, cos_ref, sin_ref, row_ref, col_ref,
    out_ref, bias, dk, dv,
):
    i, h = pl.program_id(0), pl.program_id(1)
    rows = q_ref.shape[0]
    heads = pl.num_programs(1)
    lanes, k_lanes, v_lanes = (
        pl.ds(pl.multiple_of((part * heads + h) * 128, 128), 128) for part in range(3)
    )

    @pl.when(h == 0)
    def _():
        allowed = (col_ref[0:1] <= row_ref[:, 0:1]) & (col_ref[1:2] == row_ref[:, 1:2])
        bias[...] = jnp.where(allowed, 0.0, -1e30)

    @pl.when(i == 0)
    def _():
        dk[:, lanes] = jnp.zeros((dk.shape[0], 128), f32)
        dv[:, lanes] = jnp.zeros((dv.shape[0], 128), f32)

    def turn_back(values, cosine, sine):
        return values * cosine - pltpu.roll(values, 64, 1) * sine

    q, k, v, do = q_ref[...], k_ref[...], v_ref[...], do_ref[...]
    lse = jnp.sum(jnp.where(iota((rows, 128), 1) == h, lse_ref[...], 0.0), axis=1, keepdims=True)
    delta = jnp.sum(do.astype(f32) * mixed_ref[...], axis=1, keepdims=True)
    scale = 128 ** -0.5
    scores = dot(q, k, 1, 1) * scale + bias[...]
    probs = jnp.exp(scores - lse)
    d_probs = dot(do, v, 1, 1)
    d_scores = (probs * (d_probs - delta) * scale).astype(bf16)
    dv[:, lanes] += dot(probs, do, 0, 0)
    dk[:, lanes] += dot(d_scores, q, 0, 0)
    here = pl.ds(pl.multiple_of(i * rows, rows), rows)
    d_query = dot(d_scores, k, 1, 0)
    out_ref[here, lanes] = turn_back(d_query, cos_ref[here, :], sin_ref[here, :]).astype(bf16)

    @pl.when(i == pl.num_programs(0) - 1)
    def _():
        out_ref[:, k_lanes] = turn_back(dk[:, lanes], cos_ref[...], sin_ref[...]).astype(bf16)
        out_ref[:, v_lanes] = dv[:, lanes].astype(bf16)


def rope_tables(places):
    frequency = jnp.exp(
        jnp.arange(64, dtype=f32) * (-2.0 * 9.210340371976184 / 128)
    )
    angles = places.astype(f32)[:, None] * frequency[None, :]
    cosine, sine = jnp.cos(angles), jnp.sin(angles)
    return jnp.concatenate([cosine, cosine], axis=1), jnp.concatenate([-sine, sine], axis=1)


def attention_forward(projected, cosine, sine, row_info, col_info):
    length, width = projected.shape[0], projected.shape[1] // 3
    heads, size = width // 128, min(BQ, length)
    count = length // size
    tile = pl.BlockSpec((size, 128), lambda i, h: (i, h))

    def first(part):
        return pl.BlockSpec(
            (length, 128), lambda i, h: (0, part * heads + jnp.where(i == 0, h, heads - 1))
        )

    return pl.pallas_call(
        attention_forward_kernel,
        grid=(count, heads),
        in_specs=[
            tile, first(1), first(2), whole(cosine.shape), whole(sine.shape),
            pl.BlockSpec((size, 2), lambda i, h: (i, 0)), whole(col_info.shape),
        ],
        out_specs=[
            tile, whole((length, width)), whole((length, width)), tile,
            pl.BlockSpec((size, 128), lambda i, h: (i, 0)),
        ],
        out_shape=[
            jax.ShapeDtypeStruct((length, width), bf16),
            jax.ShapeDtypeStruct((length, width), bf16),
            jax.ShapeDtypeStruct((length, width), bf16),
            jax.ShapeDtypeStruct((length, width), f32),
            jax.ShapeDtypeStruct((length, 128), f32),
        ],
        scratch_shapes=[pltpu.VMEM((size, length), f32)],
        compiler_params=pltpu.CompilerParams(vmem_limit_bytes=VMEM),
        cost_estimate=pl.CostEstimate(
            flops=4 * length * length * width, bytes_accessed=length * width * 22, transcendentals=heads * length * length
        ),
        name="attention_forward",
    )(projected, projected, projected, cosine, sine, row_info, col_info)


def attention_backward(q, k, v, do, mixed, lse, cosine, sine, row_info, col_info):
    length, width = q.shape
    heads, size = width // 128, min(BQ, length)
    count = length // size
    tile = pl.BlockSpec((size, 128), lambda i, h: (i, h))
    full = pl.BlockSpec((length, 128), lambda i, h: (0, h))
    return pl.pallas_call(
        attention_backward_kernel,
        grid=(count, heads),
        in_specs=[
            tile, full, full, tile, tile, pl.BlockSpec((size, 128), lambda i, h: (i, 0)),
            whole(cosine.shape), whole(sine.shape),
            pl.BlockSpec((size, 2), lambda i, h: (i, 0)), whole(col_info.shape),
        ],
        out_specs=whole((length, 3 * width)),
        out_shape=jax.ShapeDtypeStruct((length, 3 * width), bf16),
        scratch_shapes=[
            pltpu.VMEM((size, length), f32), pltpu.VMEM((length, width), f32), pltpu.VMEM((length, width), f32),
        ],
        compiler_params=pltpu.CompilerParams(vmem_limit_bytes=VMEM),
        cost_estimate=pl.CostEstimate(
            flops=10 * length * length * width, bytes_accessed=length * width * 16, transcendentals=heads * length * length
        ),
        name="attention_backward",
    )(q, k, v, do, mixed, lse, cosine, sine, row_info, col_info)


def gelu_backward_kernel(gu_ref, da_ref, out_ref):
    width = da_ref.shape[1]
    gate, upper, da = gu_ref[:, :width], gu_ref[:, width:], da_ref[...]
    factor = math.sqrt(2.0 / math.pi)
    bent = jnp.tanh(factor * (gate + 0.044715 * gate * gate * gate))
    slope = 0.5 * (1.0 + bent) + 0.5 * gate * (1.0 - bent * bent) * factor * (
        1.0 + 3.0 * 0.044715 * gate * gate
    )
    out_ref[:, :width] = (da * upper * slope).astype(bf16)
    out_ref[:, width:] = (da * 0.5 * gate * (1.0 + bent)).astype(bf16)


def gelu_backward(gu, da):
    length, width = da.shape
    rows = 128
    return pl.pallas_call(
        gelu_backward_kernel,
        grid=(length // rows,),
        in_specs=[
            pl.BlockSpec((rows, 2 * width), lambda i: (i, 0)),
            pl.BlockSpec((rows, width), lambda i: (i, 0)),
        ],
        out_specs=pl.BlockSpec((rows, 2 * width), lambda i: (i, 0)),
        out_shape=jax.ShapeDtypeStruct((length, 2 * width), bf16),
        compiler_params=pltpu.CompilerParams(vmem_limit_bytes=VMEM),
        cost_estimate=pl.CostEstimate(
            flops=length * width * 30, bytes_accessed=length * width * 16, transcendentals=length * width
        ),
        name="gelu_backward",
    )(gu, da)


def widen_kernel(in_ref, out_ref):
    out_ref[0] = in_ref[...].astype(f32)


def widen_parts(values, count, width):
    rows = values.shape[0]
    tile = min(rows, 512)
    return pl.pallas_call(
        widen_kernel,
        grid=(count, rows // tile),
        in_specs=[pl.BlockSpec((tile, width), lambda j, i: (i, j))],
        out_specs=pl.BlockSpec((1, tile, width), lambda j, i: (j, i, 0)),
        out_shape=jax.ShapeDtypeStruct((count, rows, width), f32),
        compiler_params=pltpu.CompilerParams(vmem_limit_bytes=VMEM),
        name="widen_parts",
    )(values)


def copy_kernel(order, in_ref, out_ref):
    out_ref[...] = in_ref[...]


def reorder(order, blocks):
    count, rows, cols = blocks.shape
    return pl.pallas_call(
        copy_kernel,
        grid_spec=pltpu.PrefetchScalarGridSpec(
            num_scalar_prefetch=1,
            grid=(count,),
            in_specs=[pl.BlockSpec((1, rows, cols), lambda i, order: (order[i], 0, 0))],
            out_specs=pl.BlockSpec((1, rows, cols), lambda i, order: (i, 0, 0)),
        ),
        out_shape=jax.ShapeDtypeStruct(blocks.shape, blocks.dtype),
        compiler_params=pltpu.CompilerParams(vmem_limit_bytes=VMEM),
        name="reorder",
    )(order, blocks)


MASKS = (0, 2, 4, 6, 1, 3, 5, 7)


class Ring:
    def __init__(self, n_seq, n_fsdp):
        self.n_seq, self.n_fsdp = n_seq, n_fsdp
        self.by_slot = n_seq == 8
        self.seq, self.fsdp = lax.axis_index("seq"), lax.axis_index("fsdp")
        places = jnp.arange(n_seq, dtype=jnp.int32)
        if self.by_slot:
            apart = places ^ self.seq
            self.order = (apart >> 1) + (apart & 1) * 4
            self.block_of_slot = jnp.array(MASKS, jnp.int32) ^ self.seq
        else:
            self.order = self.block_of_slot = places

    def swap(self, values, mask):
        return lax.ppermute(values, "seq", [(i, i ^ mask) for i in range(self.n_seq)])

    def turn(self, values, by):
        n = self.n_fsdp
        return lax.ppermute(values, "fsdp", [(i, (i + by) % n) for i in range(n)])

    def gather(self, values):
        if not self.by_slot:
            return lax.all_gather(values, "seq", axis=0, tiled=True)
        here = [values] + [self.swap(values, mask) for mask in MASKS[1:4]]
        return jnp.concatenate(here + [self.swap(block, 1) for block in here], axis=0)

    def scatter(self, away, near, length):
        if not self.by_slot:
            return [
                lax.psum_scatter(make(0, length), "seq", scatter_dimension=0, tiled=True)
                for make in near
            ]
        half, rows = length // 2, length // 8
        sent = [make(half, length).astype(bf16) for make in away]
        edges = [0]
        for part in sent:
            edges.append(edges[-1] + part.shape[1])
        spans = list(zip(edges[:-1], edges[1:]))
        arrived = self.swap(jnp.concatenate(sent, axis=1), 1)
        summed = [
            make(0, half) + arrived[:, low:high].astype(f32)
            for make, (low, high) in zip(near, spans)
        ]
        packed = jnp.concatenate([part.astype(bf16) for part in summed], axis=1)
        came = [self.swap(packed[k * rows : (k + 1) * rows], MASKS[k]) for k in (3, 1, 2)]
        return [
            sum([block[:, low:high].astype(f32) for block in came], part[:rows])
            for part, (low, high) in zip(summed, spans)
        ]

    def total_by_slot(self, values):
        if not self.by_slot:
            return lax.psum(values, "seq")
        places = jnp.arange(8, dtype=jnp.int32)[None, :]

        def pick(rows, places_of):
            chosen = (places_of[:, None] == places)[:, :, None]
            return jnp.sum(jnp.where(chosen, rows[None], 0.0), axis=1)

        total = pick(values.reshape(8, -1), self.order)
        for mask in (2, 4, 1):
            total = total + self.swap(total, mask)
        return pick(total, self.block_of_slot).reshape(values.shape)

    def total_seq(self, values):
        if not self.by_slot:
            return lax.psum(values, "seq")
        for mask in (1, 2, 4):
            values = values + self.swap(values, mask)
        return values

    def total_fsdp(self, values):
        return sum([self.turn(values, by) for by in range(1, self.n_fsdp)], values)

    def gather_fsdp(self, values):
        n = self.n_fsdp
        came = [values]
        for _ in range(n - 1):
            came.append(self.turn(came[-1], 1))
        doubled = jnp.stack((came[::-1] * 2)[:-1])
        return lax.dynamic_slice_in_dim(doubled, n - 1 - self.fsdp, n, 0)

    def scatter_fsdp(self, blocks):
        n = self.n_fsdp

        def block(back):
            place = lax.rem(self.fsdp + n - back, n)
            return lax.dynamic_index_in_dim(blocks, place, 0, False).astype(f32)

        total = block(1)
        for back in range(2, n + 1):
            total = block(back) + self.turn(total.astype(bf16), 1).astype(f32)
        return total

    def gather_all(self, values):
        rows, cols = values.shape
        along = self.gather_fsdp(values).reshape(1, -1, cols)
        if self.by_slot:
            full = reorder(self.order, self.gather(along))
        else:
            full = self.gather(along)
        return full.reshape(-1, rows, cols)


def pack(arrays, lead=0):
    parts, spans, start = [], [], 0
    for item in arrays:
        head = item.shape[:lead]
        flat = item.reshape(head + (-1,))
        rows = -(-flat.shape[-1] // 128)
        flat = jnp.pad(flat, [(0, 0)] * lead + [(0, rows * 128 - flat.shape[-1])])
        parts.append(flat.reshape(head + (rows, 128)))
        spans.append((start, rows, item.shape[lead:]))
        start += rows
    fill = -start % 16
    if fill:
        parts.append(jnp.zeros(parts[0].shape[:lead] + (fill, 128), parts[0].dtype))
    return jnp.concatenate(parts, axis=lead), spans


def unpack(packed, span):
    start, rows, shape = span
    lead = packed.shape[:-2]
    size = math.prod(shape)
    return packed[..., start : start + rows, :].reshape(lead + (-1,))[..., :size].reshape(lead + shape)


def rms_norm(values, gain):
    return values * lax.rsqrt(jnp.mean(values * values, axis=-1, keepdims=True) + epsilon) * gain


def matmul(left, right):
    return jnp.dot(left, right, preferred_element_type=f32)


def matmul_nt(left, right):
    return lax.dot_general(left, right, (((1,), (1,)), ((), ())), preferred_element_type=f32)


def matmul_tn(left, right):
    return lax.dot_general(left, right, (((0,), (0,)), ((), ())), preferred_element_type=f32)


def interleave(wide, narrow, count):
    a, b = wide.shape[1] // count, narrow.shape[1] // count
    return jnp.concatenate(
        [
            part
            for i in range(count)
            for part in (wide[:, i * a : (i + 1) * a], narrow[:, i * b : (i + 1) * b])
        ],
        axis=1,
    )


def separate(values, wide, count):
    a, step = wide // count, values.shape[1] // count
    first = [values[:, i * step : i * step + a] for i in range(count)]
    second = [values[:, i * step + a : (i + 1) * step] for i in range(count)]
    return jnp.concatenate(first, axis=1), jnp.concatenate(second, axis=1)


def side_by_side(stacked):
    return jnp.concatenate([stacked[i] for i in range(stacked.shape[0])], axis=1)


def run(
    n_seq,
    n_fsdp,
    hidden,
    embedded,
    segment,
    position,
    attn_gain,
    query_key_value_weight,
    query_key_value_down,
    query_key_value_up,
    out_weight,
    mlp_gain,
    gate_up_weight,
    feedforward_down_weight,
    feedforward_up_weight,
    down_weight,
    scan_gain,
    zx_weight,
    bc_weight,
    dt_weight,
    conv_x,
    conv_bc,
    dt_bias,
    decay_rate,
    skip_gain,
    inner_gain,
    out_proj,
    cotangent,
):
    ring = Ring(n_seq, n_fsdp)
    rows = hidden.shape[1]
    length = rows * n_seq
    attn_width = query_key_value_weight.shape[2]
    ff_width = gate_up_weight.shape[2]
    ff_rows = gate_up_weight.shape[1]
    scan_width = zx_weight.shape[2]
    scan_heads = dt_bias.shape[0]

    def scatter(*makes):
        return ring.scatter(makes, makes, length)

    def gather_weight(local, dim):
        return lax.all_gather(local, "fsdp", axis=dim, tiled=True)

    qkv_rows, out_rows, out_cols = query_key_value_weight.shape[1], *out_weight.shape
    out_cut = out_rows * out_cols // qkv_rows
    out_runs = out_cols // out_cut
    qkv_here = side_by_side(query_key_value_weight)
    out_here = jnp.concatenate(
        [out_weight[:, i * out_cut : (i + 1) * out_cut] for i in range(out_runs)]
    )
    down_rows, down_cols = down_weight.shape
    down_cut = down_rows * down_cols // qkv_rows
    down_runs = down_cols // down_cut
    down_here = jnp.concatenate(
        [down_weight[:, i * down_cut : (i + 1) * down_cut] for i in range(down_runs)]
    )
    qkv_here, out_here, down_here = lax.optimization_barrier((qkv_here, out_here, down_here))
    qkv_full = gather_weight(jnp.concatenate([qkv_here, out_here, down_here], axis=1), 0)
    edge = 3 * attn_width + out_cut
    out_full = qkv_full[:, 3 * attn_width : edge].reshape(n_fsdp, out_runs, out_rows, out_cut)
    out_full = out_full.transpose(2, 0, 1, 3).reshape(out_rows, -1)
    down_full = qkv_full[:, edge:].reshape(n_fsdp, down_runs, down_rows, down_cut)
    down_full = down_full.transpose(2, 0, 1, 3).reshape(down_rows, -1)
    qkv_full = qkv_full[:, : 3 * attn_width]
    gate_full = gather_weight(
        jnp.concatenate(
            [side_by_side(gate_up_weight), side_by_side(feedforward_up_weight)], axis=0
        ),
        0,
    )
    zx_full = gather_weight(side_by_side(zx_weight), 0)
    proj_full = gather_weight(out_proj, 1)

    packed, spans = pack(
        [
            query_key_value_down,
            feedforward_down_weight,
            bc_weight,
            attn_gain,
            mlp_gain,
            scan_gain,
            conv_bc,
        ]
    )
    everywhere = ring.gather_all(packed)
    shared = [unpack(everywhere, span) for span in spans]
    attention_down = shared[0].reshape(-1, 3 * ADAPTER_RANK)
    feedforward_down = shared[1].reshape(-1, ADAPTER_RANK)
    bc_full = shared[2].reshape(-1, 256)
    gain_one, gain_two, gain_three = (item.reshape(-1).astype(f32) for item in shared[3:6])
    taps_bc = shared[6].transpose(1, 0, 2).reshape(4, -1).astype(f32)
    packed, spans = pack(
        [query_key_value_up, dt_weight, conv_x, inner_gain]
    )
    along = ring.gather_fsdp(packed)
    shared = [unpack(along, span) for span in spans]
    qkv_up = shared[0].transpose(1, 0, 2, 3).reshape(3, ADAPTER_RANK, attn_width)
    dt_full = jnp.pad(shared[1].reshape(-1, scan_heads), ((0, 0), (0, 128 - scan_heads)))
    taps_x = shared[2].transpose(1, 0, 2).reshape(4, scan_width).astype(f32)
    inner_scale = shared[3].reshape(1, scan_width).astype(f32)
    lift = jnp.concatenate(
        [
            jnp.pad(
                qkv_up[part], ((0, 0), (part * attn_width, (2 - part) * attn_width))
            )
            for part in range(3)
        ],
        axis=0,
    )
    head_terms = jnp.pad(
        jnp.stack([dt_bias, decay_rate, skip_gain]), ((0, 5), (0, 128 - scan_heads))
    )

    marks_all = ring.gather(jnp.stack([segment[0], position[0]])[None])
    seg_slots, pos_slots = marks_all[:, 0], marks_all[:, 1]
    natural = (ring.order[:, None] == jnp.arange(n_seq)[None, :])[:, :, None]
    seg_natural = jnp.sum(jnp.where(natural, seg_slots[None], 0), axis=1).reshape(-1)
    scan_mark, scan_seg = scan_marks(seg_natural)
    places = ring.block_of_slot[:, None] * rows + jnp.arange(rows, dtype=jnp.int32)[None]
    row_info = jnp.stack([places.reshape(-1), seg_slots.reshape(-1)], axis=1).astype(f32)
    col_info = jnp.pad(row_info.T, ((0, 6), (0, 0)))
    cosine, sine = rope_tables(pos_slots.reshape(-1))

    hidden_rows = hidden[0].astype(f32)
    joined = jnp.concatenate([hidden_rows, embedded[0].astype(f32)], axis=1)
    normed, norm_pull_one = jax.vjp(rms_norm, joined, gain_one)
    normed_low = normed.astype(bf16)
    attn_rows = ring.gather(normed_low)
    lora_rows = matmul(attn_rows, attention_down).astype(bf16)
    cot_low = cotangent[0]
    cot_rows = ring.gather(cot_low)
    (
        lora_rows,
        cot_rows,
        lift,
        dt_full,
        taps_x,
        taps_bc,
        inner_scale,
        head_terms,
        scan_mark,
        scan_seg,
        row_info,
        col_info,
        cosine,
        sine,
        bc_full,
        feedforward_down,
    ) = lax.optimization_barrier(
        (
            lora_rows,
            cot_rows,
            lift,
            dt_full,
            taps_x,
            taps_bc,
            inner_scale,
            head_terms,
            scan_mark,
            scan_seg,
            row_info,
            col_info,
            cosine,
            sine,
            bc_full,
            feedforward_down,
        )
    )
    projected = matmul(attn_rows, qkv_full) + matmul(lora_rows, lift)
    query, key, value, mixed, lse = attention_forward(projected, cosine, sine, row_info, col_info)
    mixed_low = mixed.astype(bf16)
    first = hidden_rows + scatter(lambda a, b: matmul(mixed_low[a:b], out_full))[0]

    mlp_in, norm_pull_two = jax.vjp(rms_norm, first, gain_two)
    mlp_low = mlp_in.astype(bf16)
    mlp_lora_low = matmul(mlp_low, feedforward_down).astype(bf16)
    mlp_rows = ring.gather(interleave(mlp_low, mlp_lora_low, n_fsdp))
    gate_and_up = matmul(mlp_rows, gate_full)
    activated = jax.nn.gelu(gate_and_up[:, :ff_width]) * gate_and_up[:, ff_width:]
    activated_low = activated.astype(bf16)
    second = first + scatter(lambda a, b: matmul(activated_low[a:b], down_full))[0]

    scan_in, norm_pull_three = jax.vjp(rms_norm, second, gain_three)
    scan_low = scan_in.astype(bf16)
    scan_rows = ring.gather(scan_low)
    side_full = jnp.concatenate([dt_full, bc_full], axis=1)
    bc_rows = matmul(scan_rows, bc_full).astype(bf16).astype(f32)
    zx = matmul(scan_rows, zx_full)
    step_raw = matmul(scan_rows, dt_full)
    mixer, states = scan_forward(
        ring.order, zx, step_raw, bc_rows, scan_mark, scan_seg, taps_x, taps_bc, head_terms
    )
    gated = mixer * jax.nn.silu(zx[:, :scan_width])
    squares = ring.total_by_slot(jnp.sum(gated * gated, axis=1)[None])[0]
    inv_rms = lax.rsqrt(squares / DI + epsilon)
    scan_norm_low = (gated * inv_rms[:, None] * inner_scale).astype(bf16)
    proj_grad = matmul_tn(scan_norm_low, cot_rows).astype(bf16)
    proj_grad, proj_full = lax.optimization_barrier((proj_grad, proj_full))
    grad_norm = matmul_nt(cot_rows, proj_full)
    cross = ring.total_by_slot(jnp.sum(grad_norm * inner_scale * gated, axis=1)[None])[0]
    row_terms = jnp.pad(jnp.stack([inv_rms, inv_rms**3 / DI * cross]), ((0, 6), (0, 0)))
    grad_third = cot_low.astype(f32)
    g_out_proj = lax.psum_scatter(proj_grad, "fsdp", scatter_dimension=1, tiled=True)
    grad_zx, grad_side, conv_x_grad, conv_bc_grad, head_grad, inner_grad = scan_backward(
        ring.order,
        zx,
        step_raw,
        bc_rows,
        scan_mark,
        scan_seg,
        taps_x,
        taps_bc,
        head_terms,
        mixer,
        states,
        grad_norm,
        row_terms,
        inner_scale,
    )
    zx_grad = matmul_tn(scan_rows, grad_zx).astype(bf16)
    g_zx = lax.psum_scatter(zx_grad, "fsdp", scatter_dimension=0, tiled=True)
    zx_grad, grad_zx_near = lax.optimization_barrier((zx_grad, grad_zx))

    def back_of(grad):
        return lambda a, b: matmul_nt(grad[a:b], zx_full) + matmul_nt(grad_side[a:b], side_full)

    (back_three,) = ring.scatter((back_of(grad_zx),), (back_of(grad_zx_near),), length)
    back_three, g_out_proj = lax.optimization_barrier((back_three, g_out_proj))
    second_part, gain_three_grad = norm_pull_three(back_three)
    grad_second = grad_third + second_part

    second_rows = ring.gather(grad_second.astype(bf16))
    down_grad = matmul_tn(activated_low, second_rows).astype(bf16)
    down_grad, second_rows, g_zx = lax.optimization_barrier((down_grad, second_rows, g_zx))
    grad_activated = matmul_nt(second_rows, down_full)
    g_down = lax.psum_scatter(down_grad, "fsdp", scatter_dimension=1, tiled=True)
    grad_gate = gelu_backward(gate_and_up, grad_activated)
    gate_grad = matmul_tn(mlp_rows, grad_gate).astype(bf16)
    gate_grad, grad_gate_near = lax.optimization_barrier((gate_grad, grad_gate))
    g_gate = lax.psum_scatter(gate_grad, "fsdp", scatter_dimension=0, tiled=True)
    back_two = ring.scatter(
        (lambda a, b: matmul_nt(grad_gate[a:b], gate_full),),
        (lambda a, b: matmul_nt(grad_gate_near[a:b], gate_full),),
        length,
    )
    back_two, back_two_lora = separate(back_two[0], MODEL_WIDTH, n_fsdp)
    mlp_lora_grad = back_two_lora.astype(bf16)
    first_part, gain_two_grad = norm_pull_two(
        back_two + matmul_nt(mlp_lora_grad, feedforward_down)
    )
    grad_first = grad_second + first_part

    first_low, g_down = lax.optimization_barrier((grad_first.astype(bf16), g_down))
    first_rows = ring.gather(first_low)
    grad_mixed = matmul_nt(first_rows, out_full).astype(bf16)
    out_grad = matmul_tn(mixed_low, first_rows).astype(bf16)
    out_grad = out_grad.reshape(out_rows, n_fsdp, out_runs, out_cut).transpose(1, 2, 0, 3)
    out_grad = out_grad.reshape(-1, out_cut)
    grad_projected = attention_backward(
        query, key, value, grad_mixed, mixed, lse, cosine, sine, row_info, col_info
    )
    qkv_grad = matmul_tn(attn_rows, grad_projected).astype(bf16)
    qkv_grad = jnp.concatenate([qkv_grad, out_grad], axis=1)
    qkv_grad, g_gate = lax.optimization_barrier((qkv_grad, g_gate))
    g_qkv = lax.psum_scatter(qkv_grad, "fsdp", scatter_dimension=0, tiled=True)
    g_out = g_qkv[:, 3 * attn_width :].reshape(out_runs, out_rows, out_cut)
    g_out = jnp.concatenate([g_out[i] for i in range(out_runs)], axis=1)
    lift_grad = matmul_tn(lora_rows, grad_projected)
    lift_grad = jnp.stack(
        [
            lift_grad[
                part * ADAPTER_RANK : (part + 1) * ADAPTER_RANK,
                part * attn_width : (part + 1) * attn_width,
            ]
            for part in range(3)
        ]
    )
    back_one, lora_grad = scatter(
        lambda a, b: matmul_nt(grad_projected[a:b], qkv_full),
        lambda a, b: matmul_nt(grad_projected[a:b], lift),
    )
    lora_grad_low = lora_grad.astype(bf16)
    grad_joined, gain_one_grad = norm_pull_one(
        back_one + matmul_nt(lora_grad_low, attention_down)
    )
    grad_hidden = (grad_first + grad_joined[:, :MODEL_WIDTH])[None]
    grad_embedded = grad_joined[:, MODEL_WIDTH:][None]
    grad_side, lora_grad_low = lax.optimization_barrier((grad_side, lora_grad_low))
    dt_grad = matmul_tn(scan_rows, grad_side[:, :128])[:, :scan_heads]
    grad_bc_low = scatter(lambda a, b: grad_side[a:b, 128:].astype(f32))[0].astype(bf16)
    small_rows = ring.gather(
        jnp.concatenate([lora_grad_low, mlp_lora_grad, grad_bc_low], axis=1)
    )
    lora_grad_rows = small_rows[:, : 3 * ADAPTER_RANK]
    mlp_lora_grad_rows = small_rows[:, 3 * ADAPTER_RANK : 4 * ADAPTER_RANK]
    grad_bc_rows = small_rows[:, 4 * ADAPTER_RANK :]

    scan_norm_late, _ = lax.optimization_barrier((scan_norm_low, lora_grad_low))
    third = second + scatter(lambda a, b: matmul(scan_norm_late[a:b], proj_full))[0]
    output = third.astype(bf16)[None]

    def share(values_rows, grad_rows):
        wide = values_rows.shape[1] // n_seq
        cut = lax.dynamic_slice_in_dim(values_rows, ring.seq * wide, wide, 1)
        return matmul_tn(cut, grad_rows).astype(bf16).reshape(n_fsdp, wide // n_fsdp, -1)

    def share_interleaved(values_rows, grad_rows):
        wide = MODEL_WIDTH // n_seq
        runs = values_rows.reshape(length, n_fsdp, -1)[:, :, : MODEL_WIDTH // n_fsdp]
        run = lax.dynamic_index_in_dim(runs, ring.seq * n_fsdp // n_seq, 1, False)
        at = lax.rem(ring.seq, n_seq // n_fsdp) * wide
        cut = lax.dynamic_slice_in_dim(run, at, wide, 1)
        return matmul_tn(cut, grad_rows).astype(bf16).reshape(n_fsdp, wide // n_fsdp, -1)

    def by_fsdp(grad, dim):
        shape = grad.shape[:dim] + (n_fsdp, grad.shape[dim] // n_fsdp) + grad.shape[dim + 1 :]
        return jnp.moveaxis(grad.astype(bf16).reshape(shape), dim, 0)

    packed, spans = pack(
        [
            share(scan_rows, grad_bc_rows),
            by_fsdp(dt_grad, 0),
            by_fsdp(conv_x_grad[:4], 1),
            by_fsdp(inner_grad[0], 0),
            share(attn_rows, lora_grad_rows),
            by_fsdp(lift_grad, 1),
            share_interleaved(mlp_rows, mlp_lora_grad_rows),
        ],
        1,
    )
    mine = ring.scatter_fsdp(packed)
    g_bc, g_dt, g_conv_x, g_inner, g_qkv_down, g_qkv_up, g_mlp_down = (
        unpack(mine, span) for span in spans
    )
    g_heads = ring.total_fsdp(head_grad)
    g_bias, g_rate, g_skip = (g_heads[i, :scan_heads] for i in range(3))
    gains = jnp.concatenate(
        [gain_one_grad, gain_two_grad, gain_three_grad, conv_bc_grad[:4].reshape(-1)]
    )
    gains = ring.total_fsdp(ring.total_seq(gains.reshape(-1, 128))).reshape(-1)
    own = ring.seq * n_fsdp + ring.fsdp
    count = n_seq * n_fsdp

    def own_part(values):
        size = values.shape[-1] // count
        return lax.dynamic_slice_in_dim(values, own * size, size, values.ndim - 1)

    joined_width = 2 * MODEL_WIDTH
    g_attn_gain = own_part(gains[:joined_width])
    g_mlp_gain = own_part(gains[joined_width : joined_width + MODEL_WIDTH])
    g_scan_gain = own_part(gains[joined_width + MODEL_WIDTH : joined_width + 2 * MODEL_WIDTH])
    g_conv_bc = own_part(gains[joined_width + 2 * MODEL_WIDTH :].reshape(4, -1))

    def apart(grad, count):
        wide = grad.shape[1] // count
        return jnp.stack([grad[:, i * wide : (i + 1) * wide] for i in range(count)]).astype(f32)

    return (
        output,
        grad_hidden,
        grad_embedded,
        g_attn_gain,
        widen_parts(g_qkv, 3, attn_width),
        g_qkv_down,
        g_qkv_up,
        g_out.astype(f32),
        g_mlp_gain,
        apart(g_gate[:ff_rows], 2),
        g_mlp_down,
        apart(g_gate[ff_rows:], 2),
        g_down.astype(f32),
        g_scan_gain,
        apart(g_zx, 2),
        g_bc,
        g_dt,
        g_conv_x,
        g_conv_bc,
        g_bias,
        g_rate,
        g_skip,
        g_inner,
        g_out_proj.astype(f32),
    )


def solution(mesh):
    return jax.shard_map(
        functools.partial(run, mesh.shape["seq"], mesh.shape["fsdp"]),
        mesh=mesh,
        in_specs=(
            P("fsdp", "seq", None),
            P("fsdp", "seq", None),
            P("fsdp", "seq"),
            P("fsdp", "seq"),
            P(("seq", "fsdp")),
            P(None, "fsdp", "seq"),
            P(("seq", "fsdp"), None),
            P(None, "fsdp", "seq"),
            P("seq", "fsdp"),
            P(("seq", "fsdp")),
            P(None, "fsdp", "seq"),
            P(("seq", "fsdp"), None),
            P(None, "fsdp", "seq"),
            P("seq", "fsdp"),
            P(("seq", "fsdp")),
            P(None, "fsdp", "seq"),
            P(("seq", "fsdp"), None),
            P("fsdp", "seq"),
            P(None, ("seq", "fsdp")),
            P(None, ("seq", "fsdp")),
            P("seq"),
            P("seq"),
            P("seq"),
            P(("seq", "fsdp")),
            P("seq", "fsdp"),
            P("fsdp", "seq", None),
        ),
        out_specs=(
            P("fsdp", "seq", None),
            P("fsdp", "seq", None),
            P("fsdp", "seq", None),
            P(("seq", "fsdp")),
            P(None, "fsdp", "seq"),
            P(("seq", "fsdp"), None),
            P(None, "fsdp", "seq"),
            P("seq", "fsdp"),
            P(("seq", "fsdp")),
            P(None, "fsdp", "seq"),
            P(("seq", "fsdp"), None),
            P(None, "fsdp", "seq"),
            P("seq", "fsdp"),
            P(("seq", "fsdp")),
            P(None, "fsdp", "seq"),
            P(("seq", "fsdp"), None),
            P("fsdp", "seq"),
            P(None, ("seq", "fsdp")),
            P(None, ("seq", "fsdp")),
            P("seq"),
            P("seq"),
            P("seq"),
            P(("seq", "fsdp")),
            P("seq", "fsdp"),
        ),
        check_vma=False,
    )
```
